32 devices in a mesh: grp: 4 (over y, x), tok: 8 (over z, core).
Axes of the slice: x: 2, y: 2, z: 4, core: 2. Of those that a mesh axis runs over, the one named last changes fastest.
Arguments:
- hidden: bfloat16 [64, 64, 1024], P('tok', 'grp'), may hold values from -6 to 6
- draft_qkv: bfloat16 [3, 64, 64, 1024], P(None, 'tok', None, 'grp'), may hold values from -4 to 4
- self_cache: bfloat16 [64, 2, 512, 1024], P('tok', None, None, 'grp'), may hold values from -4 to 4
- cross_cache: bfloat16 [64, 2, 512, 1024], P('tok', None, None, 'grp'), may hold values from -4 to 4
- parents: int32 [64, 64], P('tok'), may hold values from -1 to 62, as said below
- counts: int32 [64], P('tok'), may hold values from 32 to 64, as said below
- self_len: int32 [64], P('tok'), may hold values from 2 to 512, as said below
- enc_len: int32 [64], P('tok'), may hold values from 2 to 512, as said below
- buckets: int32 [64, 64, 64], P('tok'), may hold values from 0 to 31
- bias_table: float32 [32, 16], P(None, 'grp'), may hold values from -4 to 4
- gain_cross: float32 [1024], replicated, may hold values from 0.25 to 1.75
- gain_ffn: float32 [1024], replicated, may hold values from 0.25 to 1.75
- gain_next: float32 [1024], replicated, may hold values from 0.25 to 1.75
- w_out_self: bfloat16 [1024, 1024], P('grp', 'tok'), may hold values from -0.1875 to 0.1875
- w_query_cross: bfloat16 [1024, 1024], P('tok', 'grp'), may hold values from -1 to 1
- w_out_cross: bfloat16 [1024, 1024], P('grp', 'tok'), may hold values from -0.1875 to 0.1875
- w_gate: bfloat16 [1024, 2816], P('tok', 'grp'), may hold values from -0.1875 to 0.1875
- w_up: bfloat16 [1024, 2816], P('tok', 'grp'), may hold values from -0.1875 to 0.1875
- w_down: bfloat16 [2816, 1024], P('grp', 'tok'), may hold values from -0.109375 to 0.109375
- w_qkv: bfloat16 [1024, 3, 1024], P('tok', None, 'grp'), may hold values from -0.1875 to 0.1875
Outputs:
- out_hidden: bfloat16 [64, 64, 1024], P('tok', 'grp')
- next_qkv: bfloat16 [3, 64, 64, 1024], P(None, 'tok', None, 'grp')
The draws below stay inside these ranges and needn't reach their ends.
Inputs may be any that keep to these rules, and one draw needn't show every extreme that they name: `parents`: slot 0 of every tree has parent -1; every other slot's parent is an earlier slot. `counts`: some request fills all 64 draft slots. `self_len`: some request fills its whole cache. `enc_len`: some request has all 512 encoder positions.
All inputs are finite; a program needn't handle non-finite values.
Results may differ from the reference program's by a relative error of at most 0.025.
Values may be sent and summed in bfloat16 or wider, within the bound.
No kernel may reach another device: no remote copies, remote signals or barrier semaphores. Data moves between devices by JAX's collectives and lax.ppermute only.
A program may use at most 64 MiB of HBM per device.

```python
import math
import jax
import jax.numpy as jnp
from jax import lax

D = 1024
H = 16
DH = 64
FF = 2816
NB = 32
DRAFT = 64
CACHE = 512
ENC = 512
REQS = 64


def draw_parents(key, part):
    raw_bits = jax.random.randint(jax.random.fold_in(key, 44), (REQS, DRAFT), 0, 1 << 20)
    slot_ids = jnp.arange(DRAFT, dtype=jnp.int32)[None, :]
    chosen = raw_bits % jnp.maximum(slot_ids, 1)
    row_ids = jnp.arange(REQS, dtype=jnp.int32)[:, None]
    chosen = jnp.where(row_ids == 0, slot_ids - 1, chosen)
    return jnp.where(slot_ids == 0, -1, chosen).astype(jnp.int32)


def draw_counts(key, part):
    drawn = jax.random.randint(jax.random.fold_in(key, 43), (REQS,), DRAFT // 2, DRAFT + 1)
    return drawn.at[0].set(DRAFT).astype(jnp.int32)


def draw_self_len(key, part):
    drawn = jax.random.randint(jax.random.fold_in(key, 41), (REQS,), 2, CACHE + 1)
    return drawn.at[0].set(CACHE).astype(jnp.int32)


def draw_enc_len(key, part):
    drawn = jax.random.randint(jax.random.fold_in(key, 42), (REQS,), 2, ENC + 1)
    return drawn.at[0].set(ENC).astype(jnp.int32)


def draw_hidden(key, part):
    own_key = jax.random.fold_in(key, 31)
    base_draw = jax.random.truncated_normal(own_key, -6.0, 6.0, (REQS, DRAFT, D), jnp.float32)
    return base_draw.astype(jnp.bfloat16)


def draw_w_query_cross(key, part):
    base_draw = jax.random.truncated_normal(jax.random.fold_in(key, 33), -4.0, 4.0, (D, D), jnp.float32) / math.sqrt(D)
    return base_draw.astype(jnp.bfloat16)


def draw_draft_qkv(key, part):
    base_draw = 0.5 * jax.random.truncated_normal(jax.random.fold_in(key, 32), -8.0, 8.0, (3, REQS, DRAFT, D), jnp.float32)
    return base_draw.astype(jnp.bfloat16)


def draw_self_cache(key, part):
    base_draw = 0.5 * jax.random.truncated_normal(jax.random.fold_in(key, 34), -8.0, 8.0, (REQS, 2, CACHE, D), jnp.float32)
    return base_draw.astype(jnp.bfloat16)


def draw_cross_cache(key, part):
    base_draw = 0.5 * jax.random.truncated_normal(jax.random.fold_in(key, 35), -8.0, 8.0, (REQS, 2, ENC, D), jnp.float32)
    return base_draw.astype(jnp.bfloat16)


def with_ends(values, key, least, largest):
    index_at = [jax.random.randint(jax.random.fold_in(key, axis), (), 0, length) for axis, length in enumerate(values.shape)]
    widest = values.shape.index(max(values.shape))
    beside = index_at[:widest] + [(index_at[widest] + 1) % values.shape[widest]] + index_at[widest + 1:]
    return values.at[tuple(index_at)].set(least).at[tuple(beside)].set(largest)


def shard_levels(stream_key, extent, pieces, low, top_value):
    level = 1.0
    for axis_at, blocks in pieces:
        draws = jax.random.uniform(jax.random.fold_in(jax.random.fold_in(stream_key, 6), axis_at), (blocks,), jnp.float32, low / len(pieces), top_value / len(pieces))
        level = level * jnp.repeat(jnp.exp(draws), extent[axis_at] // blocks).reshape((-1,) + (1,) * (len(extent) - 1 - axis_at))
    return level


def centred(key, extent, spread, limit, pieces=(), kind=jnp.bfloat16):
    values = jax.random.normal(key, extent, jnp.float32) * spread
    if len(pieces) > 0:
        values = shard_levels(key, extent, pieces, -0.22, 0.18) * values
    return jnp.clip(values, min=-limit, max=limit).astype(kind)


def setup_inputs(seed: int = 0) -> dict:
    key_of = jax.random.split(jax.random.key(seed), 21)
    hidden = draw_hidden(jax.random.fold_in(key_of[20], 71), 0)
    draft_qkv = draw_draft_qkv(jax.random.fold_in(key_of[20], 71), 0)
    self_cache = draw_self_cache(jax.random.fold_in(key_of[20], 71), 0)
    cross_cache = draw_cross_cache(jax.random.fold_in(key_of[20], 71), 0)
    parents = draw_parents(jax.random.fold_in(key_of[20], 71), 0)
    counts = draw_counts(jax.random.fold_in(key_of[20], 71), 0)
    self_len = draw_self_len(jax.random.fold_in(key_of[20], 71), 0)
    enc_len = draw_enc_len(jax.random.fold_in(key_of[20], 71), 0)
    buckets = with_ends(jax.random.randint(key_of[8], (REQS, DRAFT, DRAFT), 0, NB), jax.random.fold_in(key_of[8], 1), 0, NB - 1).astype(jnp.int32)
    bias_table = centred(key_of[9], (NB, H), 1.0, 4.0, ((1, 4),), jnp.float32)
    gain_cross = jnp.clip(1.0 + 0.15 * jax.random.normal(key_of[10], (D,), jnp.float32), 0.25, 1.75)
    gain_ffn = jnp.clip(1.0 + 0.15 * jax.random.normal(key_of[11], (D,), jnp.float32), 0.25, 1.75)
    gain_next = jnp.clip(1.0 + 0.15 * jax.random.normal(key_of[12], (D,), jnp.float32), 0.25, 1.75)
    w_out_self = centred(key_of[13], (D, D), D ** -0.5, 0.1875, ((0, 4), (1, 8)))
    w_query_cross = draw_w_query_cross(jax.random.fold_in(key_of[20], 71), 0)
    w_out_cross = centred(key_of[15], (D, D), D ** -0.5, 0.1875, ((0, 4), (1, 8)))
    w_gate = centred(key_of[16], (D, FF), D ** -0.5, 0.1875, ((0, 8), (1, 4)))
    w_up = centred(key_of[17], (D, FF), D ** -0.5, 0.1875, ((0, 8), (1, 4)))
    w_down = centred(key_of[18], (FF, D), FF ** -0.5, 0.109375, ((0, 4), (1, 8)))
    w_qkv = centred(key_of[19], (D, 3, D), D ** -0.5, 0.1875, ((0, 8), (2, 4)))
    return {"hidden": hidden, "draft_qkv": draft_qkv, "self_cache": self_cache, "cross_cache": cross_cache, "parents": parents, "counts": counts, "self_len": self_len, "enc_len": enc_len, "buckets": buckets, "bias_table": bias_table, "gain_cross": gain_cross, "gain_ffn": gain_ffn, "gain_next": gain_next, "w_out_self": w_out_self, "w_query_cross": w_query_cross, "w_out_cross": w_out_cross, "w_gate": w_gate, "w_up": w_up, "w_down": w_down, "w_qkv": w_qkv}


def ancestor_table(parent_ids):
    count_slots = parent_ids.shape[0]
    slot_ids = jnp.arange(count_slots, dtype=jnp.int32)
    ancestors = jnp.eye(count_slots, dtype=jnp.float32) + (parent_ids[:, None] == slot_ids[None, :]).astype(jnp.float32)
    for repeat in range(max(1, count_slots.bit_length())):
        ancestors = jnp.minimum(jnp.dot(ancestors, ancestors, precision=lax.Precision.HIGHEST), 1.0)
    return ancestors

def rms_scale(stream, gain_vec):
    mean_square = lax.optimization_barrier(jnp.mean(stream * stream, axis=-1, keepdims=True))
    return (stream * lax.rsqrt(mean_square + 1e-06) * gain_vec).astype(jnp.bfloat16)

def rounded_weights(values):
    return lax.optimization_barrier(values.astype(jnp.bfloat16)).astype(jnp.float32)

def draft_attention(projected, cached, parent_ids, draft_count, length, bucket_ids, bias_table):
    draft_slots = projected.shape[1]
    all_heads = bias_table.shape[1]
    head_size = projected.shape[2] // all_heads
    queries = projected[0].astype(jnp.float32).reshape(draft_slots, all_heads, head_size)
    draft_keys = projected[1].astype(jnp.float32).reshape(draft_slots, all_heads, head_size)
    draft_values = projected[2].astype(jnp.float32).reshape(draft_slots, all_heads, head_size)
    cache_keys = cached[0].astype(jnp.float32).reshape(-1, all_heads, head_size)
    cache_values = cached[1].astype(jnp.float32).reshape(-1, all_heads, head_size)
    cache_scores = jnp.einsum('ihd,phd->hip', queries, cache_keys) + bias_table[-1][:, None, None]
    cache_live = jnp.arange(cache_keys.shape[0], dtype=jnp.int32)[None, None, :] < length
    cache_scores = jnp.where(cache_live, cache_scores, -1e+30)
    draft_bias = jnp.transpose(bias_table[bucket_ids], (2, 0, 1))
    draft_scores = jnp.einsum('ihd,jhd->hij', queries, draft_keys) + draft_bias
    draft_live = (ancestor_table(parent_ids) > 0.5) & (jnp.arange(draft_slots, dtype=jnp.int32)[None, :] < draft_count)
    draft_scores = jnp.where(draft_live[None], draft_scores, -1e+30)
    highest = jnp.maximum(cache_scores.max(-1, keepdims=True), draft_scores.max(-1, keepdims=True))
    exp_cache = jnp.exp(cache_scores - highest)
    exp_draft = jnp.exp(draft_scores - highest)
    denominator = exp_cache.sum(-1, keepdims=True) + exp_draft.sum(-1, keepdims=True)
    weights_cache = rounded_weights(exp_cache / denominator)
    weights_draft = rounded_weights(exp_draft / denominator)
    attended = jnp.einsum('hip,phd->ihd', weights_cache, cache_values) + jnp.einsum('hij,jhd->ihd', weights_draft, draft_values)
    return attended.astype(jnp.bfloat16).reshape(draft_slots, -1)

def cross_attention(query_rows, cached, length):
    draft_slots = query_rows.shape[0]
    head_size = DH
    all_heads = query_rows.shape[1] // head_size
    queries = query_rows.astype(jnp.float32).reshape(draft_slots, all_heads, head_size)
    enc_keys = cached[0].astype(jnp.float32).reshape(-1, all_heads, head_size)
    enc_values = cached[1].astype(jnp.float32).reshape(-1, all_heads, head_size)
    scores = jnp.einsum('ihd,phd->hip', queries, enc_keys)
    live = jnp.arange(enc_keys.shape[0], dtype=jnp.int32)[None, None, :] < length
    scores = jnp.where(live, scores, -1e+30)
    highest = scores.max(-1, keepdims=True)
    exp_scores = jnp.exp(scores - highest)
    weights = rounded_weights(exp_scores / exp_scores.sum(-1, keepdims=True))
    attended = jnp.einsum('hip,phd->ihd', weights, enc_values)
    return attended.astype(jnp.bfloat16).reshape(draft_slots, -1)

def reference(hidden, draft_qkv, self_cache, cross_cache, parents, counts, self_len, enc_len, buckets, bias_table, gain_cross, gain_ffn, gain_next, w_out_self, w_query_cross, w_out_cross, w_gate, w_up, w_down, w_qkv):
    all_rows = REQS * DRAFT
    per_request = jnp.moveaxis(draft_qkv, 1, 0)
    self_context = lax.map(lambda request: draft_attention(request[0], request[1], request[2], request[3], request[4], request[5], bias_table), (per_request, self_cache, parents, counts, self_len, buckets))
    self_context = self_context.reshape(all_rows, D)
    stream_one = hidden.reshape(all_rows, D).astype(jnp.float32) + jnp.dot(self_context, w_out_self, preferred_element_type=jnp.float32)
    normed_one = rms_scale(stream_one, gain_cross)
    cross_query = jnp.dot(normed_one, w_query_cross, preferred_element_type=jnp.float32).astype(jnp.bfloat16)
    cross_query = cross_query.reshape(REQS, DRAFT, D)
    cross_context = lax.map(lambda request: cross_attention(request[0], request[1], request[2]), (cross_query, cross_cache, enc_len))
    cross_context = cross_context.reshape(all_rows, D)
    stream_two = stream_one + jnp.dot(cross_context, w_out_cross, preferred_element_type=jnp.float32)
    normed_two = rms_scale(stream_two, gain_ffn)
    gate_part = jnp.dot(normed_two, w_gate, preferred_element_type=jnp.float32)
    up_part = jnp.dot(normed_two, w_up, preferred_element_type=jnp.float32)
    gated = (jax.nn.gelu(gate_part, approximate=True) * up_part).astype(jnp.bfloat16)
    stream_three = stream_two + jnp.dot(gated, w_down, preferred_element_type=jnp.float32)
    out_hidden = stream_three.astype(jnp.bfloat16).reshape(REQS, DRAFT, D)
    normed_three = rms_scale(stream_three, gain_next)
    projected = jnp.dot(normed_three, w_qkv.reshape(D, 3 * D), preferred_element_type=jnp.float32).astype(jnp.bfloat16)
    next_qkv = jnp.transpose(projected.reshape(REQS, DRAFT, 3, D), (2, 0, 1, 3))
    return (out_hidden, next_qkv)
```

```python
import functools
import jax
import jax.numpy as jnp
from jax import lax
from jax.experimental import pallas as pl
from jax.experimental.pallas import tpu as pltpu
from jax.sharding import PartitionSpec as P

DH = 64
HALVES = 1
F32 = jnp.float32
BF16 = jnp.bfloat16
NEG = -1e30
VMEM_LIMIT = 48 * 1024 * 1024
ANY = pl.BlockSpec(memory_space=pl.ANY)
SMEM = pl.BlockSpec(memory_space=pltpu.SMEM)
VMEM = pl.BlockSpec(memory_space=pltpu.VMEM)


def params():
    return pltpu.CompilerParams(vmem_limit_bytes=VMEM_LIMIT)


def cost(flops, moved, transcendentals=0):
    return pl.CostEstimate(
        flops=int(flops), bytes_accessed=int(moved), transcendentals=int(transcendentals)
    )


def dot_nt(lhs, rhs):
    return lax.dot_general(lhs, rhs, (((1,), (1,)), ((), ())), preferred_element_type=F32)


def dot(lhs, rhs):
    return jnp.dot(lhs, rhs, preferred_element_type=F32)


def bias_kernel(parents_ref, counts_ref, buckets_ref, table_ref, out_ref):
    requests, slots = parents_ref.shape
    heads = out_ref.shape[1] // slots
    row = lax.broadcasted_iota(jnp.int32, (slots, slots), 0)
    col = lax.broadcasted_iota(jnp.int32, (slots, slots), 1)
    reach = []
    for r in range(requests):
        linked = (row == parents_ref[r : r + 1, :]) | (row == col)
        reach.append(jnp.where(linked, 1.0, 0.0).astype(BF16))
    span = 1
    while span < slots - 1:
        reach = [jnp.minimum(dot(a, a), 1.0).astype(BF16) for a in reach]
        span *= 2
    eye = jnp.where(row == col, 1.0, 0.0).astype(BF16)
    for r in range(requests):
        ancestors = dot_nt(eye, reach[r])
        live = (ancestors > 0.5) & (col < counts_ref[r])
        picked = buckets_ref[r]
        for h in range(heads):
            shift = table_ref[table_ref.shape[0] - 1, h]
            bias = jnp.zeros((slots, slots), F32)
            for b in range(table_ref.shape[0] - 1):
                bias = jnp.where(picked == b, table_ref[b, h] - shift, bias)
            out_ref[r, h * slots : (h + 1) * slots, :] = jnp.where(live, bias, NEG)


def draft_bias(parents, counts, buckets, bias_table):
    requests, slots = parents.shape
    heads = bias_table.shape[1]
    return pl.pallas_call(
        bias_kernel,
        out_shape=jax.ShapeDtypeStruct((requests, heads * slots, slots), F32),
        in_specs=[VMEM, SMEM, VMEM, SMEM],
        out_specs=VMEM,
        compiler_params=params(),
        cost_estimate=cost(6e7, 1.2e6),
        name="draft_bias",
    )(parents, counts, buckets, bias_table)


def spread_heads(queries, heads):
    head_of = lax.broadcasted_iota(jnp.int32, queries.shape, 1) // DH
    return jnp.concatenate(
        [jnp.where(head_of == h, queries, jnp.zeros_like(queries)) for h in range(heads)], axis=0
    )


def gather_heads(attended, heads):
    slots = attended.shape[0] // heads
    head_of = lax.broadcasted_iota(jnp.int32, (slots, attended.shape[1]), 1) // DH
    total = attended[:slots]
    for h in range(1, heads):
        total = jnp.where(head_of == h, attended[h * slots : (h + 1) * slots], total)
    return total.astype(BF16)


def self_kernel(length_ref, qkv_ref, cache_ref, bias_ref, out_ref):
    r = pl.program_id(0)
    width = qkv_ref.shape[-1]
    heads = width // DH
    queries = spread_heads(qkv_ref[0, 0], heads)
    scores = dot_nt(queries, cache_ref[0, 0])
    position = lax.broadcasted_iota(jnp.int32, (1, scores.shape[1]), 1)
    scores = jnp.where(position < length_ref[r], scores, NEG)
    draft = dot_nt(queries, qkv_ref[1, 0]) + bias_ref[0]
    highest = jnp.maximum(scores.max(-1, keepdims=True), draft.max(-1, keepdims=True))
    scores = jnp.exp(scores - highest)
    draft = jnp.exp(draft - highest)
    total = scores.sum(-1, keepdims=True) + draft.sum(-1, keepdims=True)
    attended = dot(scores.astype(BF16), cache_ref[0, 1]) + dot(draft.astype(BF16), qkv_ref[2, 0])
    out_ref[0] = gather_heads(attended / total, heads)


def self_attention(draft_qkv, cache, bias, length):
    _, requests, slots, width = draft_qkv.shape
    depth = cache.shape[2]
    return pl.pallas_call(
        self_kernel,
        grid=(requests,),
        out_shape=jax.ShapeDtypeStruct((requests, slots, width), BF16),
        in_specs=[
            SMEM,
            pl.BlockSpec((3, 1, slots, width), lambda r: (0, r, 0, 0)),
            pl.BlockSpec((1, 2, depth, width), lambda r: (r, 0, 0, 0)),
            pl.BlockSpec((1, bias.shape[1], slots), lambda r: (r, 0, 0)),
        ],
        out_specs=pl.BlockSpec((1, slots, width), lambda r: (r, 0, 0)),
        compiler_params=params(),
        cost_estimate=cost(5e9, 6e6, 1.2e6),
        name="self_attention",
    )(length, draft_qkv, cache, bias)


def self_out_kernel(ways, first, place_ref, ctx_ref, w_ref, hidden_ref, own_ref, *out_refs):
    share = hidden_ref.shape[1]
    count = own_ref.shape[0] // share
    width = ctx_ref.shape[-1]
    for k in list(range(1, ways)) + [0]:
        owner = jnp.bitwise_xor(place_ref[0], k)
        start = pl.multiple_of(owner * share, share)
        rows = ctx_ref[pl.ds(first, count), pl.ds(start, share), :].reshape(count * share, width)
        part = dot(rows, w_ref[...])
        if k == 0:
            base = hidden_ref[pl.ds(first, count)].reshape(count * share, -1)
            own_ref[...] = part + base.astype(F32)
        else:
            out_refs[k - 1][...] = part.astype(BF16)


def self_out(place, ctx, w, hidden, ways, first, count):
    share, model = hidden.shape[1], hidden.shape[2]
    rows = count * share
    return pl.pallas_call(
        functools.partial(self_out_kernel, ways, first),
        out_shape=[jax.ShapeDtypeStruct((rows, model), F32)]
        + [jax.ShapeDtypeStruct((rows, model), BF16)] * (ways - 1),
        in_specs=[SMEM, VMEM, VMEM, VMEM],
        out_specs=[VMEM] * ways,
        compiler_params=params(),
        cost_estimate=cost(2 * rows * ways * ctx.shape[-1] * model, 2e6),
        name="self_out",
    )(place, ctx, w, hidden)


def norm_kernel(own_ref, *refs):
    others = refs[:-3]
    gain_ref, stream_ref, normed_ref = refs[-3:]
    stream = own_ref[...]
    for other in others:
        stream = stream + other[...].astype(F32)
    stream_ref[...] = stream.astype(stream_ref.dtype)
    scale = lax.rsqrt(jnp.mean(stream * stream, axis=-1, keepdims=True) + 1e-06)
    normed_ref[...] = (stream * scale * gain_ref[...]).astype(BF16)


def norm(own, others, gain, kept=F32):
    return pl.pallas_call(
        norm_kernel,
        out_shape=[
            jax.ShapeDtypeStruct(own.shape, kept),
            jax.ShapeDtypeStruct(own.shape, BF16),
        ],
        in_specs=[VMEM] * (len(others) + 2),
        out_specs=[VMEM] * 2,
        compiler_params=params(),
        cost_estimate=cost(1e6, 2e6),
        name="norm",
    )(own, *others, gain.reshape(1, -1))


def cross_kernel(ways, first, length_ref, *refs):
    blocks = refs[:ways]
    wq_ref, cache_ref, wo_ref, stream_ref = refs[ways : ways + 4]
    own_ref = refs[ways + 4]
    out_refs = refs[ways + 5 : 2 * ways + 4]
    query_ref, ctx_ref = refs[-2:]
    r = pl.program_id(0)
    width = wq_ref.shape[1]
    heads = width // DH
    rows = blocks[0].shape[0]
    share = rows // pl.num_programs(0)

    @pl.when(r == 0)
    def _():
        for k in range(ways):
            query_ref[k] = dot(blocks[k][...], wq_ref[...]).astype(BF16)

    start = pl.multiple_of(r * share, share)
    queries = query_ref[:, pl.ds(start, share), :].reshape(ways * share, width)
    scores = dot_nt(spread_heads(queries, heads), cache_ref[0, 0])
    position = lax.broadcasted_iota(jnp.int32, (1, scores.shape[1]), 1)
    scores = jnp.where(position < length_ref[r + first], scores, NEG)
    scores = jnp.exp(scores - scores.max(-1, keepdims=True))
    total = scores.sum(-1, keepdims=True)
    attended = dot(scores.astype(BF16), cache_ref[0, 1])
    ctx = gather_heads(attended / total, heads)
    ctx_ref[:, pl.ds(start, share), :] = ctx.reshape(ways, share, width)

    @pl.when(r == pl.num_programs(0) - 1)
    def _():
        for k in range(ways):
            part = dot(ctx_ref[k], wo_ref[...])
            if k == 0:
                own_ref[...] = part + stream_ref[...]
            else:
                out_refs[k - 1][...] = part.astype(BF16)


def cross_layer(blocks, wq, cache, wo, stream, length, first, count):
    ways = len(blocks)
    rows, model = blocks[0].shape
    depth, width = cache.shape[2], cache.shape[3]
    full = lambda shape: pl.BlockSpec(shape, lambda r: (0,) * len(shape))
    return pl.pallas_call(
        functools.partial(cross_kernel, ways, first),
        grid=(count,),
        out_shape=[jax.ShapeDtypeStruct((rows, model), F32)]
        + [jax.ShapeDtypeStruct((rows, model), BF16)] * (ways - 1),
        in_specs=[SMEM]
        + [full((rows, model))] * ways
        + [
            full(wq.shape),
            pl.BlockSpec((1, 2, depth, width), lambda r: (r + first, 0, 0, 0)),
            full(wo.shape),
            full((rows, model)),
        ],
        out_specs=[full((rows, model))] * ways,
        scratch_shapes=[pltpu.VMEM((ways, rows, width), BF16), pltpu.VMEM((ways, rows, width), BF16)],
        compiler_params=params(),
        cost_estimate=cost(2.5e9 * count / 4, 4e6 * count / 4, 6e5),
        name="cross_layer",
    )(length, *blocks, wq, cache, wo, stream)


def ffn_kernel(ways, *refs):
    blocks = refs[:ways]
    wgu_ref, wd_ref, stream_ref, own_ref = refs[ways : ways + 4]
    out_refs = refs[ways + 4 :]
    hidden = wd_ref.shape[0]
    for k in list(range(1, ways)) + [0]:
        both = dot(blocks[k][...], wgu_ref[...])
        gated = (jax.nn.gelu(both[:, :hidden], approximate=True) * both[:, hidden:]).astype(BF16)
        part = dot(gated, wd_ref[...])
        if k == 0:
            own_ref[...] = part + stream_ref[...]
        else:
            out_refs[k - 1][...] = part.astype(BF16)


def ffn(blocks, wgu, wd, stream):
    ways = len(blocks)
    rows, model = blocks[0].shape
    return pl.pallas_call(
        functools.partial(ffn_kernel, ways),
        out_shape=[jax.ShapeDtypeStruct((rows, model), F32)]
        + [jax.ShapeDtypeStruct((rows, model), BF16)] * (ways - 1),
        in_specs=[VMEM] * (ways + 3),
        out_specs=[VMEM] * ways,
        compiler_params=params(),
        cost_estimate=cost(2 * rows * ways * (wgu.size + wd.size), 6e6, 4e5),
        name="ffn",
    )(*blocks, wgu, wd, stream)


def project_kernel(ways, place_ref, *refs):
    blocks, w_ref, out_ref = refs[:ways], refs[ways], refs[ways + 1]
    _, count, slots, width = out_ref.shape
    share = slots // ways
    for k in range(ways):
        projected = dot(blocks[k][...], w_ref[...]).astype(BF16)
        start = pl.multiple_of(jnp.bitwise_xor(place_ref[0], k) * share, share)
        for c in range(3):
            piece = projected[:, c * width : (c + 1) * width].reshape(count, share, width)
            out_ref[c, :, pl.ds(start, share), :] = piece


def project(place, blocks, w, count, share):
    ways = len(blocks)
    rows = blocks[0].shape[0]
    return pl.pallas_call(
        functools.partial(project_kernel, ways),
        out_shape=jax.ShapeDtypeStruct((3, count, share * ways, w.shape[1] // 3), BF16),
        in_specs=[SMEM] + [VMEM] * (ways + 1),
        out_specs=VMEM,
        compiler_params=params(),
        cost_estimate=cost(2 * rows * ways * w.size, 4e6),
        name="project",
    )(place, *blocks, w)


def place_kernel(plan, shapes, place_ref, *refs):
    pieces = refs[: len(refs) - len(shapes) - 1]
    outs = refs[len(pieces) : -1]
    sem = refs[-1]
    copies = []
    for k, piece in enumerate(pieces):
        source = jnp.bitwise_xor(place_ref[1], k)
        for out, row, rows, by_row, col in plan:
            if by_row:
                target = outs[out].at[pl.ds(pl.multiple_of(source * rows, rows), rows), col]
            else:
                lanes = piece.shape[1]
                target = outs[out].at[:, pl.ds(pl.multiple_of(source * lanes, lanes), lanes)]
            copies.append(
                pltpu.make_async_copy(
                    piece.at[pl.ds(row, rows), :], target, sem.at[len(copies)]
                )
            )
    for copy in copies:
        copy.start()
    for copy in copies:
        copy.wait()


def place_pieces(place, pieces, plan, shapes):
    return pl.pallas_call(
        functools.partial(place_kernel, plan, shapes),
        out_shape=[jax.ShapeDtypeStruct(shape, BF16) for shape in shapes],
        in_specs=[SMEM] + [ANY] * len(pieces),
        out_specs=[ANY] * len(shapes),
        scratch_shapes=[pltpu.SemaphoreType.DMA((len(pieces) * len(plan),))],
        compiler_params=params(),
        cost_estimate=cost(1e3, 2 * len(pieces) * pieces[0].size * 2),
        name="place_pieces",
    )(place, *pieces)


def fetch(shard, total):
    pieces = []
    for k in range(0, total, 2):
        here = shard
        if k:
            here = lax.ppermute(shard, "tok", [(i, i ^ k) for i in range(total)])
        there = lax.ppermute(here, "tok", [(i, i ^ 1) for i in range(total)])
        pieces += [here, there]
    return pieces


def gather_weights(place, total, w_out_self, w_query, w_out_cross, w_gate, w_up, w_down, w_qkv):
    model_slice = w_query.shape[0]
    hidden = w_gate.shape[1]
    w_qkv = w_qkv.reshape(w_qkv.shape[0], -1)
    w_gate_up = jnp.concatenate([w_gate, w_up], axis=1)
    if total != 8 or model_slice != 128 or w_out_self.shape[1] != 128:
        by_row = functools.partial(lax.all_gather, axis_name="tok", axis=0, tiled=True)
        by_col = functools.partial(lax.all_gather, axis_name="tok", axis=1, tiled=True)
        return (
            by_col(w_out_self),
            by_row(w_query),
            by_col(w_out_cross),
            by_row(w_gate_up),
            by_col(w_down),
            by_row(w_qkv),
        )
    model = model_slice * total
    head_width = w_query.shape[1]
    everything = slice(None)
    (out_self,) = place_pieces(
        place, fetch(w_out_self, total), [(0, 0, head_width, False, None)], [(head_width, model)]
    )
    packed = jnp.concatenate([w_query[:, :128], w_query[:, 128:], w_out_cross], axis=0)
    query, out_cross = place_pieces(
        place,
        fetch(packed, total),
        [
            (0, 0, 128, True, pl.ds(0, 128)),
            (0, 128, 128, True, pl.ds(128, 128)),
            (1, 256, head_width, False, None),
        ],
        [(model, head_width), (head_width, model)],
    )
    (gate_up,) = place_pieces(
        place, fetch(w_gate_up, total), [(0, 0, 128, True, everything)], [(model, 2 * hidden)]
    )
    (down,) = place_pieces(
        place, fetch(w_down, total), [(0, 0, hidden, False, None)], [(hidden, model)]
    )
    (qkv,) = place_pieces(
        place, fetch(w_qkv, total), [(0, 0, 128, True, everything)], [(model, w_qkv.shape[1])]
    )
    return out_self, query, out_cross, gate_up, down, qkv


def send_each(parts, ways):
    return [
        lax.ppermute(part, "grp", [(i, i ^ k) for i in range(ways)])
        for k, part in zip(range(1, ways), parts)
    ]


def spread(block, ways):
    return [block] + send_each([block] * (ways - 1), ways)


def shards(
    ways,
    total,
    hidden,
    draft_qkv,
    self_cache,
    cross_cache,
    parents,
    counts,
    self_len,
    enc_len,
    buckets,
    bias_table,
    gain_cross,
    gain_ffn,
    gain_next,
    w_out_self,
    w_query_cross,
    w_out_cross,
    w_gate,
    w_up,
    w_down,
    w_qkv,
):
    requests, share, model = hidden.shape
    count = requests // HALVES
    place = jnp.stack([lax.axis_index("grp"), lax.axis_index("tok")]).astype(jnp.int32)
    out_self, query, out_cross, gate_up, down, qkv = gather_weights(
        place, total, w_out_self, w_query_cross, w_out_cross, w_gate, w_up, w_down, w_qkv
    )
    bias = draft_bias(parents, counts, buckets, bias_table)
    ctx = self_attention(draft_qkv, self_cache, bias, self_len)
    hidden_parts, qkv_parts = [], []
    for part in range(HALVES):
        first = part * count
        own, *parts = self_out(place, ctx, out_self, hidden, ways, first, count)
        stream, normed = norm(own, send_each(parts, ways), gain_cross)
        own, *parts = cross_layer(
            spread(normed, ways), query, cross_cache, out_cross, stream, enc_len, first, count
        )
        stream, normed = norm(own, send_each(parts, ways), gain_ffn)
        own, *parts = ffn(spread(normed, ways), gate_up, down, stream)
        stream, normed = norm(own, send_each(parts, ways), gain_next, BF16)
        hidden_parts.append(stream.reshape(count, share, model))
        qkv_parts.append(project(place, spread(normed, ways), qkv, count, share))
    if HALVES == 1:
        return hidden_parts[0], qkv_parts[0]
    return jnp.concatenate(hidden_parts, axis=0), jnp.concatenate(qkv_parts, axis=1)


def solution(mesh):
    in_specs = (
        P("tok", "grp", None),
        P(None, "tok", None, "grp"),
        P("tok", None, None, "grp"),
        P("tok", None, None, "grp"),
        P("tok", None),
        P("tok"),
        P("tok"),
        P("tok"),
        P("tok", None, None),
        P(None, "grp"),
        P(),
        P(),
        P(),
        P("grp", "tok"),
        P("tok", "grp"),
        P("grp", "tok"),
        P("tok", "grp"),
        P("tok", "grp"),
        P("grp", "tok"),
        P("tok", None, "grp"),
    )
    out_specs = (P("tok", "grp", None), P(None, "tok", None, "grp"))
    body = functools.partial(shards, mesh.shape["grp"], mesh.shape["tok"])
    return jax.shard_map(body, mesh=mesh, in_specs=in_specs, out_specs=out_specs, check_vma=False)
```

```python
import functools
import jax
import jax.numpy as jnp
from jax import lax
from jax.experimental import pallas as pl
from jax.experimental.pallas import tpu as pltpu
from jax.sharding import PartitionSpec as P

DH = 64
F32 = jnp.float32
BF16 = jnp.bfloat16
NEG = -1e30
MIB = 1024 * 1024
HBM = pl.BlockSpec(memory_space=pl.ANY)
SMEM = pl.BlockSpec(memory_space=pltpu.SMEM)
VMEM = pl.BlockSpec(memory_space=pltpu.VMEM)


def params(limit=28):
    return pltpu.CompilerParams(vmem_limit_bytes=limit * MIB)


def cost(flops, moved, transcendentals=0):
    return pl.CostEstimate(
        flops=int(flops), bytes_accessed=int(moved), transcendentals=int(transcendentals)
    )


def dot_nt(lhs, rhs):
    return lax.dot_general(lhs, rhs, (((1,), (1,)), ((), ())), preferred_element_type=F32)


def dot(lhs, rhs):
    return jnp.dot(lhs, rhs, preferred_element_type=F32)


def ancestor_masks(parents_ref, counts_ref):
    requests, slots = parents_ref.shape
    row = lax.broadcasted_iota(jnp.int32, (slots, slots), 0)
    col = lax.broadcasted_iota(jnp.int32, (slots, slots), 1)
    reach = []
    for r in range(requests):
        linked = (row == parents_ref[r : r + 1, :]) | (row == col)
        reach.append(jnp.where(linked, 1.0, 0.0).astype(BF16))
    span = 1
    while span < slots - 1:
        reach = [jnp.minimum(dot(a, a), 1.0).astype(BF16) for a in reach]
        span *= 2
    eye = jnp.where(row == col, 1.0, 0.0).astype(BF16)
    return [
        (dot_nt(eye, reach[r]) > 0.5) & (col < counts_ref[r]) for r in range(requests)
    ]


def bias_rows(table_ref):
    heads, kinds = table_ref.shape
    shifted = table_ref[...] - table_ref[:, kinds - 1 :]
    return jnp.concatenate([shifted, jnp.zeros((heads, 128 - kinds), F32)], axis=1)


def draft_bias(live, picked, table):
    slots, lanes = live.shape[0], table.shape[1]
    picked = jnp.concatenate([picked, jnp.zeros((slots, lanes - slots), jnp.int32)], axis=1)
    parts = []
    for h in range(table.shape[0]):
        row_of = jnp.broadcast_to(table[h : h + 1, :], (slots, lanes))
        bias = jnp.take_along_axis(row_of, picked, axis=1)[:, :slots]
        parts.append(jnp.where(live, bias, NEG))
    return jnp.concatenate(parts, axis=0)


def spread_heads(queries, heads):
    head_of = lax.broadcasted_iota(jnp.int32, queries.shape, 1) // DH
    return jnp.concatenate(
        [jnp.where(head_of == h, queries, jnp.zeros_like(queries)) for h in range(heads)], axis=0
    )


def gather_heads(attended, heads):
    slots = attended.shape[0] // heads
    head_of = lax.broadcasted_iota(jnp.int32, (slots, attended.shape[1]), 1) // DH
    total = attended[:slots]
    for h in range(1, heads):
        total = jnp.where(head_of == h, attended[h * slots : (h + 1) * slots], total)
    return total.astype(BF16)


def fetch_requests(pairs, sems):
    copies = []
    for r in range(pairs[0][1].shape[0]):
        copies.append([])
        for at, (source, target) in enumerate(pairs):
            copy = pltpu.make_async_copy(source(r), target.at[r], sems.at[r, at])
            copy.start()
            copies[r].append(copy)
    return copies


def self_kernel(
    counts_ref, length_ref, parents_ref, buckets_ref, table_ref, qkv_hbm, cache_hbm, out_ref,
    qkv_ref, cache_ref, sems,
):
    requests, slots, width = out_ref.shape
    heads = width // DH
    copies = fetch_requests(
        [(lambda r: cache_hbm.at[r], cache_ref), (lambda r: qkv_hbm.at[:, r], qkv_ref)], sems
    )
    live = ancestor_masks(parents_ref, counts_ref)
    table = bias_rows(table_ref)
    position = lax.broadcasted_iota(jnp.int32, (1, cache_ref.shape[2]), 1)
    for r in range(requests):
        for copy in copies[r]:
            copy.wait()
        queries = spread_heads(qkv_ref[r, 0], heads)
        scores = dot_nt(queries, cache_ref[r, 0])
        scores = jnp.where(position < length_ref[r], scores, NEG)
        draft = dot_nt(queries, qkv_ref[r, 1]) + draft_bias(live[r], buckets_ref[r], table)
        highest = jnp.maximum(scores.max(-1, keepdims=True), draft.max(-1, keepdims=True))
        scores = jnp.exp(scores - highest)
        draft = jnp.exp(draft - highest)
        total = scores.sum(-1, keepdims=True) + draft.sum(-1, keepdims=True)
        attended = dot(scores.astype(BF16), cache_ref[r, 1])
        attended = attended + dot(draft.astype(BF16), qkv_ref[r, 2])
        out_ref[r] = gather_heads(attended / total, heads)


def self_attention(draft_qkv, cache, parents, counts, buckets, bias_table, length):
    _, requests, slots, width = draft_qkv.shape
    return pl.pallas_call(
        self_kernel,
        out_shape=jax.ShapeDtypeStruct((requests, slots, width), BF16),
        in_specs=[SMEM, SMEM, VMEM, VMEM, VMEM, HBM, HBM],
        out_specs=VMEM,
        scratch_shapes=[
            pltpu.VMEM((requests, 3, slots, width), BF16),
            pltpu.VMEM(cache.shape, BF16),
            pltpu.SemaphoreType.DMA((requests, 2)),
        ],
        compiler_params=params(60),
        cost_estimate=cost(5e9, 6e6, 1.2e6),
        name="self_attention",
    )(counts, length, parents, buckets, bias_table.T, draft_qkv, cache)


def columns(ref, place_ref, pieces, j):
    lanes = ref.shape[-1] // pieces
    return pl.ds(pl.multiple_of(jnp.bitwise_xor(place_ref[1], j) * lanes, lanes), lanes)


def each_slice(stacks, orders):
    for stack, order in zip(stacks, orders):
        for at, k in enumerate(order):
            yield k, stack.at[at]


def join_columns(out_ref, slices, first, rows):
    for k, piece in slices:
        lanes = piece.shape[1]
        out_ref[:, k * lanes : (k + 1) * lanes] = piece[first : first + rows, :]


def self_out_kernel(ways, orders, place_ref, *refs):
    stacks = refs[: len(orders)]
    ctx_ref, hidden_ref, own_ref = refs[len(orders) : len(orders) + 3]
    out_refs = refs[-ways:-1]
    w_ref = refs[-1]
    pieces = sum(len(order) for order in orders)
    requests, share, model = hidden_ref.shape
    width = w_ref.shape[0]
    join_columns(w_ref, each_slice(stacks, orders), 0, width)
    for k in list(range(ways - 1, 0, -1)) + [0]:
        owner = jnp.bitwise_xor(place_ref[0], k)
        start = pl.multiple_of(owner * share, share)
        rows = ctx_ref[:, pl.ds(start, share), :]
        part = dot(rows.reshape(requests * share, width), w_ref[...])
        if k == 0:
            lanes = model // pieces
            for j in range(pieces):
                base = hidden_ref[:, :, columns(hidden_ref, place_ref, pieces, j)]
                base = base.astype(F32).reshape(requests * share, lanes)
                here = slice(j * lanes, (j + 1) * lanes)
                own_ref[:, here] = part[:, here] + base
        else:
            out_refs[k - 1][...] = part.astype(BF16)


def self_out(place, ctx, stacks, orders, hidden, ways):
    requests, share, model = hidden.shape
    rows = requests * share
    width = ctx.shape[2]
    return pl.pallas_call(
        functools.partial(self_out_kernel, ways, orders),
        out_shape=[jax.ShapeDtypeStruct((rows, model), F32)]
        + [jax.ShapeDtypeStruct((rows, model), BF16)] * (ways - 1),
        in_specs=[SMEM] + [VMEM] * (len(stacks) + 2),
        out_specs=[VMEM] * ways,
        scratch_shapes=[pltpu.VMEM((width, model), BF16)],
        compiler_params=params(),
        cost_estimate=cost(2 * rows * ways * width * model, 2e6),
        name="self_out",
    )(place, *stacks, ctx, hidden)


def norm_kernel(pieces, last, place_ref, own_ref, *refs):
    others = refs[:-3]
    gain_ref, stream_ref, normed_ref = refs[-3:]
    stream = own_ref[...]
    for other in others:
        stream = stream + other[...].astype(F32)
    lanes = stream.shape[1] // pieces
    scale = lax.rsqrt(jnp.mean(stream * stream, axis=-1, keepdims=True) + 1e-06)
    for j in range(pieces):
        here = slice(j * lanes, (j + 1) * lanes)
        there = columns(gain_ref, place_ref, pieces, j)
        stream_ref[:, there if last else here] = stream[:, here].astype(stream_ref.dtype)
        normed_ref[:, here] = (stream[:, here] * scale * gain_ref[:, there]).astype(BF16)


def norm(place, own, others, gain, pieces, last=False):
    return pl.pallas_call(
        functools.partial(norm_kernel, pieces, last),
        out_shape=[
            jax.ShapeDtypeStruct(own.shape, BF16 if last else F32),
            jax.ShapeDtypeStruct(own.shape, BF16),
        ],
        in_specs=[SMEM] + [VMEM] * (len(others) + 2),
        out_specs=[VMEM] * 2,
        compiler_params=params(),
        cost_estimate=cost(1e6, 2e6),
        name="norm",
    )(place, own, *others, gain.reshape(1, -1))


def cross_kernel(ways, orders, length_ref, cache_hbm, stream_ref, *refs):
    blocks = refs[:ways]
    stacks = refs[ways : -(ways + 5)]
    own_ref = refs[-(ways + 5)]
    out_refs = refs[-(ways + 4) : -5]
    wq_ref, wo_ref, ctx_ref, cache_ref, sems = refs[-5:]
    requests = cache_ref.shape[0]
    width = wq_ref.shape[1]
    heads = width // DH
    rows = blocks[0].shape[0]
    share = rows // requests
    copies = fetch_requests([(lambda r: cache_hbm.at[r], cache_ref)], sems)
    if orders:
        lanes = stacks[0].shape[2]
        parts = width // lanes
        for k, piece in each_slice(stacks, orders):
            for c in range(parts):
                here = slice(c * lanes, (c + 1) * lanes)
                at = width + c * lanes
                wq_ref[k * lanes : (k + 1) * lanes, here] = piece[at : at + lanes, :]
        join_columns(wo_ref, each_slice(stacks, orders), width + parts * lanes, width)
    else:
        wq_ref[...] = stacks[0][...]
        wo_ref[...] = stacks[1][...]
    query = [dot(block[...], wq_ref[...]).astype(BF16) for block in blocks]
    position = lax.broadcasted_iota(jnp.int32, (1, cache_ref.shape[2]), 1)
    for r in range(requests):
        for copy in copies[r]:
            copy.wait()
        here = slice(r * share, (r + 1) * share)
        queries = spread_heads(jnp.concatenate([q[here] for q in query], axis=0), heads)
        scores = dot_nt(queries, cache_ref[r, 0])
        scores = jnp.where(position < length_ref[r], scores, NEG)
        scores = jnp.exp(scores - scores.max(-1, keepdims=True))
        total = scores.sum(-1, keepdims=True)
        attended = dot(scores.astype(BF16), cache_ref[r, 1])
        ctx = gather_heads(attended / total, heads)
        ctx_ref[:, here, :] = ctx.reshape(ways, share, width)
    for k in list(range(ways - 1, 0, -1)) + [0]:
        part = dot(ctx_ref[k], wo_ref[...])
        if k == 0:
            own_ref[...] = part + stream_ref[...]
        else:
            out_refs[k - 1][...] = part.astype(BF16)


def cross_layer(blocks, stacks, orders, cache, stream, length):
    ways = len(blocks)
    rows, model = blocks[0].shape
    width = cache.shape[3]
    return pl.pallas_call(
        functools.partial(cross_kernel, ways, orders),
        out_shape=[jax.ShapeDtypeStruct((rows, model), F32)]
        + [jax.ShapeDtypeStruct((rows, model), BF16)] * (ways - 1),
        in_specs=[SMEM, HBM] + [VMEM] * (1 + ways + len(stacks)),
        out_specs=[VMEM] * ways,
        scratch_shapes=[
            pltpu.VMEM((model, width), BF16),
            pltpu.VMEM((width, model), BF16),
            pltpu.VMEM((ways, rows, width), BF16),
            pltpu.VMEM(cache.shape, BF16),
            pltpu.SemaphoreType.DMA((cache.shape[0], 1)),
        ],
        compiler_params=params(54),
        cost_estimate=cost(5e9, 8e6, 1.2e6),
        name="cross_layer",
    )(length, cache, stream, *blocks, *stacks)


def join_kernel(place_ref, slices_ref, out_ref):
    pieces, _, lanes = slices_ref.shape
    for k in range(pieces):
        source = jnp.bitwise_xor(place_ref[1], k)
        out_ref[:, k * lanes : (k + 1) * lanes] = slices_ref[source]


def join(place, slices):
    pieces, rows, lanes = slices.shape
    return pl.pallas_call(
        join_kernel,
        out_shape=jax.ShapeDtypeStruct((rows, lanes * pieces), BF16),
        in_specs=[SMEM, VMEM],
        out_specs=VMEM,
        compiler_params=params(),
        cost_estimate=cost(1e3, 4 * rows * lanes * pieces),
        name="join",
    )(place, slices)


def ffn_kernel(block_ref, w_ref, *refs):
    hidden = w_ref.shape[0] // 3
    gate = dot_nt(block_ref[...], w_ref[:hidden, :])
    up = dot_nt(block_ref[...], w_ref[hidden : 2 * hidden, :])
    gated = (jax.nn.gelu(gate, approximate=True) * up).astype(BF16)
    part = dot(gated, w_ref[2 * hidden :, :])
    if len(refs) == 2:
        part = part + refs[0][...]
    refs[-1][...] = part.astype(refs[-1].dtype)


def ffn(block, w, stream=None):
    rows, model = block.shape
    given = [] if stream is None else [stream]
    return pl.pallas_call(
        ffn_kernel,
        out_shape=jax.ShapeDtypeStruct((rows, model), F32 if given else BF16),
        in_specs=[VMEM] * (2 + len(given)),
        out_specs=VMEM,
        compiler_params=params(),
        cost_estimate=cost(2 * rows * w.size, 6e6, 1e5),
        name="ffn",
    )(block, w, *given)


def project_kernel(ways, place_ref, *refs):
    blocks, slices_ref, out_ref, w_ref = refs[:ways], *refs[ways:]
    _, count, slots, width = out_ref.shape
    share = slots // ways
    pieces, _, depth, _ = slices_ref.shape
    for k in range(pieces):
        source = jnp.bitwise_xor(place_ref[1], k) if pieces > 1 else 0
        w_ref[:, k * depth : (k + 1) * depth, :] = slices_ref[source]
    for k in range(ways):
        start = pl.multiple_of(jnp.bitwise_xor(place_ref[0], k) * share, share)
        for c in range(3):
            projected = dot(blocks[k][...], w_ref[c]).astype(BF16)
            out_ref[c, :, pl.ds(start, share), :] = projected.reshape(count, share, width)


def project(place, blocks, slices, count, share):
    ways = len(blocks)
    rows, model = blocks[0].shape
    width = slices.shape[3]
    return pl.pallas_call(
        functools.partial(project_kernel, ways),
        out_shape=jax.ShapeDtypeStruct((3, count, share * ways, width), BF16),
        in_specs=[SMEM] + [VMEM] * (ways + 1),
        out_specs=VMEM,
        scratch_shapes=[pltpu.VMEM((3, model, width), BF16)],
        compiler_params=params(),
        cost_estimate=cost(6 * rows * ways * model * width, 4e6),
        name="project",
    )(place, *blocks, slices)


ATTN_ORDERS = ((0, 4, 6, 2), (1, 5, 7, 3))


def gate(*values):
    return lax.optimization_barrier(values)


def partner(value, axis, size, k):
    return lax.ppermute(value, axis, [(i, i ^ k) for i in range(size)])


def all_slices(shard):
    return lax.all_gather(shard, "tok", axis=0, tiled=False)


def along(value, k):
    return partner(value, "tok", 8, k)


def send_each(parts, ways):
    return [partner(part, "grp", ways, k) for k, part in zip(range(1, ways), parts)]


def spread(block, ways):
    return [block] + send_each([block] * (ways - 1), ways)


def shards(
    ways,
    total,
    hidden,
    draft_qkv,
    self_cache,
    cross_cache,
    parents,
    counts,
    self_len,
    enc_len,
    buckets,
    bias_table,
    gain_cross,
    gain_ffn,
    gain_next,
    w_out_self,
    w_query_cross,
    w_out_cross,
    w_gate,
    w_up,
    w_down,
    w_qkv,
):
    requests, share, model = hidden.shape
    slice_lanes = model // total
    head_width = w_query_cross.shape[1]
    place = jnp.stack([lax.axis_index("grp"), lax.axis_index("tok")]).astype(jnp.int32)
    paired = total == 8 and slice_lanes == 128 and head_width % slice_lanes == 0
    qkv_shard = jnp.transpose(w_qkv, (1, 0, 2))
    if not paired:
        by_row = functools.partial(lax.all_gather, axis_name="tok", axis=0, tiled=True)
        by_col = functools.partial(lax.all_gather, axis_name="tok", axis=1, tiled=True)
        whole = ((0,),)
        ctx = self_attention(draft_qkv, self_cache, parents, counts, buckets, bias_table, self_len)
        own, *parts = self_out(place, ctx, [by_col(w_out_self)[None]], whole, hidden, ways)
        stream, normed = norm(place, own, send_each(parts, ways), gain_cross, 1)
        attn_w = [by_row(w_query_cross), by_col(w_out_cross)]
        own, *parts = cross_layer(spread(normed, ways), attn_w, (), cross_cache, stream, enc_len)
        stream, normed = norm(place, own, send_each(parts, ways), gain_ffn, 1)
        ffn_w = jnp.concatenate([by_row(w_gate).T, by_row(w_up).T, by_col(w_down)], axis=0)
        others = spread(normed, ways)[1:]
        own = ffn(normed, ffn_w, stream)
        parts = [ffn(block, ffn_w) for block in others]
        stream, normed = norm(place, own, send_each(parts, ways), gain_next, 1, True)
        qkv_w = by_col(qkv_shard)[None]
        next_qkv = project(place, spread(normed, ways), qkv_w, requests, share)
        return stream.reshape(requests, share, model), next_qkv

    pieces = total
    query_slices = jnp.split(w_query_cross, head_width // slice_lanes, axis=1)
    attn_shard = jnp.concatenate([w_out_self] + query_slices + [w_out_cross], axis=0)
    ffn_shard = jnp.concatenate([w_gate.T, w_up.T, w_down], axis=0)
    attn_here = [attn_shard] + [along(attn_shard, k) for k in (4, 6, 2)]
    ctx = self_attention(draft_qkv, self_cache, parents, counts, buckets, bias_table, self_len)
    ctx, ffn_shard, qkv_shard, *attn_here = gate(ctx, ffn_shard, qkv_shard, *attn_here)
    ffn_w = all_slices(ffn_shard)
    attn_here = jnp.stack(attn_here)
    attn_w = [attn_here, along(attn_here, 1)]
    own, *parts = self_out(place, ctx, attn_w, ATTN_ORDERS, hidden, ways)
    own, qkv_shard, *parts = gate(own, qkv_shard, *parts)
    qkv_w = all_slices(qkv_shard)
    stream, normed = norm(place, own, send_each(parts, ways), gain_cross, pieces)
    blocks = spread(normed, ways)
    own, *parts = cross_layer(blocks, attn_w, ATTN_ORDERS, cross_cache, stream, enc_len)
    stream, normed = norm(place, own, send_each(parts, ways), gain_ffn, pieces)
    blocks = spread(normed, ways)
    ffn_w = join(place, ffn_w)
    own = ffn(normed, ffn_w, stream)
    parts = [ffn(block, ffn_w) for block in blocks[1:]]
    stream, normed = norm(place, own, send_each(parts, ways), gain_next, pieces, True)
    blocks = spread(normed, ways)
    next_qkv = project(place, blocks, qkv_w, requests, share)
    return stream.reshape(requests, share, model), next_qkv


def solution(mesh):
    in_specs = (
        P("tok", "grp", None),
        P(None, "tok", None, "grp"),
        P("tok", None, None, "grp"),
        P("tok", None, None, "grp"),
        P("tok", None),
        P("tok"),
        P("tok"),
        P("tok"),
        P("tok", None, None),
        P(None, "grp"),
        P(),
        P(),
        P(),
        P("grp", "tok"),
        P("tok", "grp"),
        P("grp", "tok"),
        P("tok", "grp"),
        P("tok", "grp"),
        P("grp", "tok"),
        P("tok", None, "grp"),
    )
    out_specs = (P("tok", "grp", None), P(None, "tok", None, "grp"))
    body = functools.partial(shards, mesh.shape["grp"], mesh.shape["tok"])
    return jax.shard_map(body, mesh=mesh, in_specs=in_specs, out_specs=out_specs, check_vma=False)
```

```python
import functools
import jax
import jax.numpy as jnp
from jax import lax
from jax.experimental import pallas as pl
from jax.experimental.pallas import tpu as pltpu
from jax.sharding import PartitionSpec as P

DH = 64
HALVES = 2
F32 = jnp.float32
BF16 = jnp.bfloat16
NEG = -1e30
MIB = 1024 * 1024
CROSS_LIMIT = 28
HBM = pl.BlockSpec(memory_space=pl.ANY)
SMEM = pl.BlockSpec(memory_space=pltpu.SMEM)
VMEM = pl.BlockSpec(memory_space=pltpu.VMEM)


def params(limit=28):
    return pltpu.CompilerParams(vmem_limit_bytes=limit * MIB)


def cost(flops, moved, transcendentals=0):
    return pl.CostEstimate(
        flops=int(flops), bytes_accessed=int(moved), transcendentals=int(transcendentals)
    )


def dot_nt(lhs, rhs):
    return lax.dot_general(lhs, rhs, (((1,), (1,)), ((), ())), preferred_element_type=F32)


def dot(lhs, rhs):
    return jnp.dot(lhs, rhs, preferred_element_type=F32)


def ancestor_masks(parents_ref, counts_ref):
    requests, slots = parents_ref.shape
    row = lax.broadcasted_iota(jnp.int32, (slots, slots), 0)
    col = lax.broadcasted_iota(jnp.int32, (slots, slots), 1)
    reach = []
    for r in range(requests):
        linked = (row == parents_ref[r : r + 1, :]) | (row == col)
        reach.append(jnp.where(linked, 1.0, 0.0).astype(BF16))
    span = 1
    while span < slots - 1:
        reach = [jnp.minimum(dot(a, a), 1.0).astype(BF16) for a in reach]
        span *= 2
    eye = jnp.where(row == col, 1.0, 0.0).astype(BF16)
    return [(dot_nt(eye, reach[r]) > 0.5) & (col < counts_ref[r]) for r in range(requests)]


def draft_biases(parents_ref, counts_ref, buckets_ref, table_ref):
    requests, slots = parents_ref.shape
    heads, kinds = table_ref.shape
    lanes = 2 * slots
    live = ancestor_masks(parents_ref, counts_ref)
    shifted = table_ref[...] - table_ref[:, kinds - 1 :]
    table = jnp.concatenate([shifted, jnp.zeros((heads, lanes - kinds), F32)], axis=1)
    biases = [[] for _ in range(requests)]
    for r in range(0, requests, 2):
        picked = jnp.concatenate([buckets_ref[r], buckets_ref[r + 1]], axis=1)
        for h in range(heads):
            row_of = jnp.broadcast_to(table[h : h + 1, :], (slots, lanes))
            both = jnp.take_along_axis(row_of, picked, axis=1)
            biases[r].append(jnp.where(live[r], both[:, :slots], NEG))
            biases[r + 1].append(jnp.where(live[r + 1], both[:, slots:], NEG))
    return [jnp.concatenate(parts, axis=0) for parts in biases]


def spread_heads(queries, heads):
    head_of = lax.broadcasted_iota(jnp.int32, queries.shape, 1) // DH
    return jnp.concatenate(
        [jnp.where(head_of == h, queries, jnp.zeros_like(queries)) for h in range(heads)], axis=0
    )


def gather_heads(attended, heads):
    slots = attended.shape[0] // heads
    head_of = lax.broadcasted_iota(jnp.int32, (slots, attended.shape[1]), 1) // DH
    total = attended[:slots]
    for h in range(1, heads):
        total = jnp.where(head_of == h, attended[h * slots : (h + 1) * slots], total)
    return total.astype(BF16)


def bias_kernel(parents_ref, counts_ref, buckets_ref, table_ref, out_ref):
    for r, bias in enumerate(draft_biases(parents_ref, counts_ref, buckets_ref, table_ref)):
        out_ref[r] = bias


def bias_and_mask(parents, counts, buckets, bias_table):
    requests, slots = parents.shape
    heads = bias_table.shape[1]
    return pl.pallas_call(
        bias_kernel,
        out_shape=jax.ShapeDtypeStruct((requests, heads * slots, slots), F32),
        in_specs=[VMEM, SMEM, VMEM, VMEM],
        out_specs=VMEM,
        compiler_params=params(60),
        cost_estimate=cost(6e7, 1.2e6),
        name="bias_and_mask",
    )(parents, counts, buckets, bias_table.T)


def self_kernel(length_ref, qkv_ref, cache_ref, bias_ref, out_ref):
    step, width = out_ref.shape[0], out_ref.shape[2]
    heads = width // DH
    position = lax.broadcasted_iota(jnp.int32, (1, cache_ref.shape[2]), 1)
    for s in range(step):
        length = length_ref[pl.program_id(0) * step + s]
        queries = spread_heads(qkv_ref[0, s], heads)
        scores = dot_nt(queries, cache_ref[s, 0])
        scores = jnp.where(position < length, scores, NEG)
        draft = dot_nt(queries, qkv_ref[1, s]) + bias_ref[s]
        highest = jnp.maximum(scores.max(-1, keepdims=True), draft.max(-1, keepdims=True))
        scores = jnp.exp(scores - highest)
        draft = jnp.exp(draft - highest)
        total = scores.sum(-1, keepdims=True) + draft.sum(-1, keepdims=True)
        attended = dot(scores.astype(BF16), cache_ref[s, 1])
        attended = attended + dot(draft.astype(BF16), qkv_ref[2, s])
        out_ref[s] = gather_heads(attended / total, heads)


def self_attention(draft_qkv, cache, length, bias):
    _, requests, slots, width = draft_qkv.shape
    step = requests // HALVES
    depth = cache.shape[2]
    return pl.pallas_call(
        self_kernel,
        grid=(HALVES,),
        out_shape=jax.ShapeDtypeStruct((requests, slots, width), BF16),
        in_specs=[
            SMEM,
            pl.BlockSpec((3, step, slots, width), lambda h: (0, h, 0, 0)),
            pl.BlockSpec((step, 2, depth, width), lambda h: (h, 0, 0, 0)),
            pl.BlockSpec((step, bias.shape[1], slots), lambda h: (h, 0, 0)),
        ],
        out_specs=pl.BlockSpec((step, slots, width), lambda h: (h, 0, 0)),
        compiler_params=params(60),
        cost_estimate=cost(5e9, 6e6, 1.2e6),
        name="self_attention",
    )(length, draft_qkv, cache, bias)


def columns(ref, pieces, j):
    lanes = ref.shape[-1] // pieces
    return pl.ds(pl.multiple_of(jnp.bitwise_xor(lax.axis_index("tok"), j) * lanes, lanes), lanes)


def each_slice(stacks, orders):
    for stack, order in zip(stacks, orders):
        for at, k in enumerate(order):
            yield k, stack.at[at]


def join_columns(out_ref, slices, first, rows):
    for k, piece in slices:
        lanes = piece.shape[1]
        out_ref[:, k * lanes : (k + 1) * lanes] = piece[first : first + rows, :]


def self_out_kernel(ways, orders, first, *refs):
    stacks = refs[: len(orders)]
    ctx_ref, hidden_ref, own_ref = refs[len(orders) : len(orders) + 3]
    out_refs = refs[-ways:-1]
    w_ref = refs[-1]
    pieces = sum(len(order) for order in orders)
    width = ctx_ref.shape[2]
    share, model = hidden_ref.shape[1:]
    rows = own_ref.shape[0]
    requests = rows // share
    join_columns(w_ref, each_slice(stacks, orders), 0, width)
    taken = []
    for k in range(ways):
        owner = jnp.bitwise_xor(lax.axis_index("grp"), k)
        start = pl.multiple_of(owner * share, share)
        taken.append(
            ctx_ref[first : first + requests, pl.ds(start, share), :].reshape(rows, width)
        )
    part = dot(jnp.concatenate(taken, axis=0), w_ref[...])
    for k in range(1, ways):
        out_refs[k - 1][...] = part[k * rows : (k + 1) * rows].astype(BF16)
    lanes = model // pieces
    for j in range(pieces):
        base = hidden_ref[first : first + requests, :, columns(hidden_ref, pieces, j)]
        here = slice(j * lanes, (j + 1) * lanes)
        own_ref[:, here] = part[:rows, here] + base.astype(F32).reshape(rows, lanes)


def self_out(ctx, stacks, orders, hidden, ways, first, count):
    width = ctx.shape[2]
    share, model = hidden.shape[1:]
    rows = count * share
    return pl.pallas_call(
        functools.partial(self_out_kernel, ways, orders, first),
        out_shape=[jax.ShapeDtypeStruct((rows, model), F32)]
        + [jax.ShapeDtypeStruct((rows, model), BF16)] * (ways - 1),
        in_specs=[VMEM] * (len(stacks) + 2),
        out_specs=[VMEM] * ways,
        scratch_shapes=[pltpu.VMEM((width, model), BF16)],
        compiler_params=params(),
        cost_estimate=cost(2 * rows * ways * width * model, 2e6),
        name="self_out",
    )(*stacks, ctx, hidden)


def norm_kernel(pieces, last, own_ref, *refs):
    others = refs[:-3]
    gain_ref, stream_ref, normed_ref = refs[-3:]
    stream = own_ref[...]
    for other in others:
        stream = stream + other[...].astype(F32)
    lanes = stream.shape[1] // pieces
    scale = lax.rsqrt(jnp.mean(stream * stream, axis=-1, keepdims=True) + 1e-06)
    for j in range(pieces):
        here = slice(j * lanes, (j + 1) * lanes)
        there = columns(gain_ref, pieces, j)
        stream_ref[:, there if last else here] = stream[:, here].astype(stream_ref.dtype)
        normed_ref[:, here] = (stream[:, here] * scale * gain_ref[:, there]).astype(BF16)


def norm(own, others, gain, pieces, last=False):
    return pl.pallas_call(
        functools.partial(norm_kernel, pieces, last),
        out_shape=[
            jax.ShapeDtypeStruct(own.shape, BF16 if last else F32),
            jax.ShapeDtypeStruct(own.shape, BF16),
        ],
        in_specs=[VMEM] * (len(others) + 2),
        out_specs=[VMEM] * 2,
        compiler_params=params(),
        cost_estimate=cost(1e6, 2e6),
        name="norm",
    )(own, *others, gain.reshape(1, -1))


def cross_kernel(ways, first, length_ref, cache_ref, stream_ref, *refs):
    blocks = refs[:ways]
    given = refs[ways : -(ways + 3)]
    own_ref = refs[-(ways + 3)]
    out_refs = refs[-(ways + 2) : -3]
    wq_ref, wo_ref, ctx_ref = refs[-3:]
    requests = cache_ref.shape[0]
    width = wq_ref.shape[1]
    heads = width // DH
    rows = blocks[0].shape[0]
    share = rows // requests
    if len(given) == 1:
        (slices_ref,) = given
        pieces, _, lanes = slices_ref.shape
        parts = width // lanes
        for k in range(pieces):
            piece = slices_ref.at[jnp.bitwise_xor(lax.axis_index("tok"), k)]
            for c in range(parts):
                here = slice(c * lanes, (c + 1) * lanes)
                block = piece[c * lanes : (c + 1) * lanes, :]
                wq_ref[k * lanes : (k + 1) * lanes, here] = block
            wo_ref[:, k * lanes : (k + 1) * lanes] = piece[parts * lanes :, :]
    else:
        wq_ref[...] = given[0][...]
        wo_ref[...] = given[1][...]
    normed = jnp.concatenate([block[...] for block in blocks], axis=0)
    query = dot(normed, wq_ref[...]).astype(BF16).reshape(ways, rows, width)
    position = lax.broadcasted_iota(jnp.int32, (1, cache_ref.shape[2]), 1)
    for r in range(requests):
        here = slice(r * share, (r + 1) * share)
        queries = spread_heads(query[:, here].reshape(ways * share, width), heads)
        scores = dot_nt(queries, cache_ref[r, 0])
        scores = jnp.where(position < length_ref[first + r], scores, NEG)
        scores = jnp.exp(scores - scores.max(-1, keepdims=True))
        total = scores.sum(-1, keepdims=True)
        attended = dot(scores.astype(BF16), cache_ref[r, 1])
        ctx = gather_heads(attended / total, heads)
        ctx_ref[:, here, :] = ctx.reshape(ways, share, width)
    part = dot(ctx_ref[...].reshape(ways * rows, width), wo_ref[...])
    own_ref[...] = part[:rows] + stream_ref[...]
    for k in range(1, ways):
        out_refs[k - 1][...] = part[k * rows : (k + 1) * rows].astype(BF16)


def cross_layer(blocks, weights, cache, stream, length, first, count):
    ways = len(blocks)
    rows, model = blocks[0].shape
    depth, width = cache.shape[2:]
    full = lambda shape: pl.BlockSpec(shape, lambda i: (0,) * len(shape))
    return pl.pallas_call(
        functools.partial(cross_kernel, ways, first),
        grid=(1,),
        out_shape=[jax.ShapeDtypeStruct((rows, model), F32)]
        + [jax.ShapeDtypeStruct((rows, model), BF16)] * (ways - 1),
        in_specs=[
            SMEM,
            pl.BlockSpec((count, 2, depth, width), lambda i: (first // count, 0, 0, 0)),
            full((rows, model)),
        ]
        + [full((rows, model))] * ways
        + [full(weight.shape) for weight in weights],
        out_specs=[full((rows, model))] * ways,
        scratch_shapes=[
            pltpu.VMEM((model, width), BF16),
            pltpu.VMEM((width, model), BF16),
            pltpu.VMEM((ways, rows, width), BF16),
        ],
        compiler_params=params(CROSS_LIMIT),
        cost_estimate=cost(5e9 * count / 8, 8e6 * count / 8, 1.2e6 * count / 8),
        name="cross_layer",
    )(length, cache, stream, *blocks, *weights)


def join_kernel(slices_ref, out_ref):
    pieces, _, lanes = slices_ref.shape
    for k in range(pieces):
        source = jnp.bitwise_xor(lax.axis_index("tok"), k)
        out_ref[:, k * lanes : (k + 1) * lanes] = slices_ref[source]


def join(slices):
    pieces, rows, lanes = slices.shape
    return pl.pallas_call(
        join_kernel,
        out_shape=jax.ShapeDtypeStruct((rows, lanes * pieces), BF16),
        in_specs=[VMEM],
        out_specs=VMEM,
        compiler_params=params(),
        cost_estimate=cost(1e3, 4 * rows * lanes * pieces),
        name="join",
    )(slices)


def ffn_kernel(ways, w_ref, stream_ref, *refs):
    blocks, own_ref, out_refs = refs[:ways], refs[ways], refs[ways + 1 :]
    hidden = w_ref.shape[0] // 3
    rows = stream_ref.shape[0]
    normed = jnp.concatenate([block[...] for block in blocks], axis=0)
    gate = dot_nt(normed, w_ref[:hidden, :])
    up = dot_nt(normed, w_ref[hidden : 2 * hidden, :])
    gated = (jax.nn.gelu(gate, approximate=True) * up).astype(BF16)
    part = dot(gated, w_ref[2 * hidden :, :])
    own_ref[...] = part[:rows] + stream_ref[...]
    for k in range(1, ways):
        out_refs[k - 1][...] = part[k * rows : (k + 1) * rows].astype(BF16)


def ffn(blocks, w, stream):
    ways = len(blocks)
    rows, model = stream.shape
    return pl.pallas_call(
        functools.partial(ffn_kernel, ways),
        out_shape=[jax.ShapeDtypeStruct((rows, model), F32)]
        + [jax.ShapeDtypeStruct((rows, model), BF16)] * (ways - 1),
        in_specs=[VMEM] * (2 + ways),
        out_specs=[VMEM] * ways,
        compiler_params=params(),
        cost_estimate=cost(2 * rows * ways * w.size, 6e6, 4e5),
        name="ffn",
    )(w, stream, *blocks)


def project_kernel(ways, first, slices_ref, *refs):
    blocks, out_hbm, w_ref, made_ref, sem = refs[:ways], *refs[-4:]
    _, count, slots, width = made_ref.shape
    share = slots // ways
    pieces, _, depth, _ = slices_ref.shape
    for k in range(pieces):
        source = jnp.bitwise_xor(lax.axis_index("tok"), k) if pieces > 1 else 0
        w_ref[:, k * depth : (k + 1) * depth, :] = slices_ref[source]
    normed = jnp.concatenate([block[...] for block in blocks], axis=0)
    for c in range(3):
        projected = dot(normed, w_ref[c]).astype(BF16).reshape(ways, count, share, width)
        for k in range(ways):
            start = pl.multiple_of(jnp.bitwise_xor(lax.axis_index("grp"), k) * share, share)
            made_ref[c, :, pl.ds(start, share), :] = projected[k]
    copy = pltpu.make_async_copy(made_ref, out_hbm.at[:, first : first + count], sem)
    copy.start()
    copy.wait()


def project(blocks, slices, requests, share, first, count, base):
    ways = len(blocks)
    model = blocks[0].shape[1]
    width = slices.shape[3]
    given = [] if base is None else [base]
    return pl.pallas_call(
        functools.partial(project_kernel, ways, first),
        out_shape=jax.ShapeDtypeStruct((3, requests, share * ways, width), BF16),
        in_specs=[VMEM] * (ways + 1) + [HBM] * len(given),
        out_specs=HBM,
        scratch_shapes=[
            pltpu.VMEM((3, model, width), BF16),
            pltpu.VMEM((3, count, share * ways, width), BF16),
            pltpu.SemaphoreType.DMA,
        ],
        input_output_aliases={ways + 1: 0} if given else {},
        compiler_params=params(),
        cost_estimate=cost(6 * count * share * ways * model * width, 4e6),
        name="project",
    )(slices, *blocks, *given)


ATTN_ORDERS = ((0, 4, 6, 2), (1, 5, 7, 3))


def gate(*values):
    return lax.optimization_barrier(values)


def partner(value, axis, size, k):
    return lax.ppermute(value, axis, [(i, i ^ k) for i in range(size)])


def all_slices(shard):
    return lax.all_gather(shard, "tok", axis=0, tiled=False)


def along(value, k):
    return partner(value, "tok", 8, k)


def send_each(parts, ways):
    return [partner(part, "grp", ways, k) for k, part in zip(range(1, ways), parts)]


def spread(block, ways):
    return [block] + send_each([block] * (ways - 1), ways)


def shards(
    ways,
    total,
    hidden,
    draft_qkv,
    self_cache,
    cross_cache,
    parents,
    counts,
    self_len,
    enc_len,
    buckets,
    bias_table,
    gain_cross,
    gain_ffn,
    gain_next,
    w_out_self,
    w_query_cross,
    w_out_cross,
    w_gate,
    w_up,
    w_down,
    w_qkv,
):
    requests, share, model = hidden.shape
    slice_lanes = model // total
    head_width = w_query_cross.shape[1]
    paired = total == 8 and slice_lanes == 128 and head_width % slice_lanes == 0
    qkv_shard = jnp.transpose(w_qkv, (1, 0, 2))
    halves = range(HALVES)
    count = requests // HALVES
    starts = [h * count for h in halves]
    bias = bias_and_mask(parents, counts, buckets, bias_table)
    ctx = self_attention(draft_qkv, self_cache, self_len, bias)
    if paired:
        pieces, orders = total, ATTN_ORDERS
        query_slices = jnp.split(w_query_cross, head_width // slice_lanes, axis=1)
        attn_w = [all_slices(jnp.concatenate(query_slices + [w_out_cross], axis=0))]
        out_here = [w_out_self] + [along(w_out_self, k) for k in (4, 6, 2)]
        ctx, out_here = gate(ctx, out_here)
        out_here = jnp.stack(out_here)
        out_w = [out_here, along(out_here, 1)]
        out_here, w_gate, w_up, w_down, qkv_shard = gate(
            out_here, w_gate, w_up, w_down, qkv_shard
        )
        ffn_w = all_slices(jnp.concatenate([w_gate.T, w_up.T, w_down], axis=0))
    else:
        pieces = 1
        by_row = functools.partial(lax.all_gather, axis_name="tok", axis=0, tiled=True)
        by_col = functools.partial(lax.all_gather, axis_name="tok", axis=1, tiled=True)
        out_w, orders = [by_col(w_out_self)[None]], ((0,),)
        attn_w = [by_row(w_query_cross), by_col(w_out_cross)]
        ffn_w = jnp.concatenate([by_row(w_gate).T, by_row(w_up).T, by_col(w_down)], axis=0)
        qkv_w = by_col(qkv_shard)[None]
    made = [self_out(ctx, out_w, orders, hidden, ways, start, count) for start in starts]
    if paired:
        *made[-1], qkv_shard = gate(*made[-1], qkv_shard)
        qkv_w = all_slices(qkv_shard)
    sent = [send_each(made[h][1:], ways) for h in halves]
    kept = [norm(made[h][0], sent[h], gain_cross, pieces) for h in halves]
    blocks = [spread(kept[h][1], ways) for h in halves]
    made = [
        cross_layer(blocks[h], attn_w, cross_cache, kept[h][0], enc_len, starts[h], count)
        for h in halves
    ]
    sent = [send_each(made[h][1:], ways) for h in halves]
    kept = [norm(made[h][0], sent[h], gain_ffn, pieces) for h in halves]
    blocks = [spread(kept[h][1], ways) for h in halves]
    if paired:
        ffn_w = join(ffn_w)
    made = [ffn(blocks[h], ffn_w, kept[h][0]) for h in halves]
    sent = [send_each(made[h][1:], ways) for h in halves]
    kept = [norm(made[h][0], sent[h], gain_next, pieces, True) for h in halves]
    blocks = [spread(kept[h][1], ways) for h in halves]
    next_qkv = None
    for h in halves:
        next_qkv = project(blocks[h], qkv_w, requests, share, starts[h], count, next_qkv)
    out_hidden = jnp.concatenate([kept[h][0] for h in halves], axis=0)
    return out_hidden.reshape(requests, share, model), next_qkv


def solution(mesh):
    in_specs = (
        P("tok", "grp", None),
        P(None, "tok", None, "grp"),
        P("tok", None, None, "grp"),
        P("tok", None, None, "grp"),
        P("tok", None),
        P("tok"),
        P("tok"),
        P("tok"),
        P("tok", None, None),
        P(None, "grp"),
        P(),
        P(),
        P(),
        P("grp", "tok"),
        P("tok", "grp"),
        P("grp", "tok"),
        P("tok", "grp"),
        P("tok", "grp"),
        P("grp", "tok"),
        P("tok", None, "grp"),
    )
    out_specs = (P("tok", "grp", None), P(None, "tok", None, "grp"))
    body = functools.partial(shards, mesh.shape["grp"], mesh.shape["tok"])
    return jax.shard_map(body, mesh=mesh, in_specs=in_specs, out_specs=out_specs, check_vma=False)
```

```python
import functools
import jax
import jax.numpy as jnp
from jax import lax
from jax.experimental import pallas as pl
from jax.experimental.pallas import tpu as pltpu
from jax.sharding import PartitionSpec as P

DH = 64
HALVES = 2
F32 = jnp.float32
BF16 = jnp.bfloat16
NEG = -1e30
MIB = 1024 * 1024
CROSS_LIMIT = 28
HBM = pl.BlockSpec(memory_space=pl.ANY)
SMEM = pl.BlockSpec(memory_space=pltpu.SMEM)
VMEM = pl.BlockSpec(memory_space=pltpu.VMEM)


def params(limit=28):
    return pltpu.CompilerParams(vmem_limit_bytes=limit * MIB)


def cost(flops, moved, transcendentals=0):
    return pl.CostEstimate(
        flops=int(flops), bytes_accessed=int(moved), transcendentals=int(transcendentals)
    )


def dot_nt(lhs, rhs):
    return lax.dot_general(lhs, rhs, (((1,), (1,)), ((), ())), preferred_element_type=F32)


def dot(lhs, rhs):
    return jnp.dot(lhs, rhs, preferred_element_type=F32)


def ancestor_masks(parents_ref, counts_ref):
    requests, slots = parents_ref.shape
    row = lax.broadcasted_iota(jnp.int32, (slots, slots), 0)
    col = lax.broadcasted_iota(jnp.int32, (slots, slots), 1)
    reach = []
    for r in range(requests):
        linked = (row == parents_ref[r : r + 1, :]) | (row == col)
        reach.append(jnp.where(linked, 1.0, 0.0).astype(BF16))
    span = 1
    while span < slots - 1:
        reach = [jnp.minimum(dot(a, a), 1.0).astype(BF16) for a in reach]
        span *= 2
    eye = jnp.where(row == col, 1.0, 0.0).astype(BF16)
    return [(dot_nt(eye, reach[r]) > 0.5) & (col < counts_ref[r]) for r in range(requests)]


def draft_biases(parents_ref, counts_ref, buckets_ref, table_ref):
    requests, slots = parents_ref.shape
    heads, kinds = table_ref.shape
    lanes = 2 * slots
    live = ancestor_masks(parents_ref, counts_ref)
    shifted = table_ref[...] - table_ref[:, kinds - 1 :]
    table = jnp.concatenate([shifted, jnp.zeros((heads, lanes - kinds), F32)], axis=1)
    biases = [[] for _ in range(requests)]
    for r in range(0, requests, 2):
        picked = jnp.concatenate([buckets_ref[r], buckets_ref[r + 1]], axis=1)
        for h in range(heads):
            row_of = jnp.broadcast_to(table[h : h + 1, :], (slots, lanes))
            both = jnp.take_along_axis(row_of, picked, axis=1)
            biases[r].append(jnp.where(live[r], both[:, :slots], NEG))
            biases[r + 1].append(jnp.where(live[r + 1], both[:, slots:], NEG))
    return [jnp.concatenate(parts, axis=0) for parts in biases]


def spread_heads(queries, heads):
    head_of = lax.broadcasted_iota(jnp.int32, queries.shape, 1) // DH
    return jnp.concatenate(
        [jnp.where(head_of == h, queries, jnp.zeros_like(queries)) for h in range(heads)], axis=0
    )


def gather_heads(attended, heads):
    slots = attended.shape[0] // heads
    head_of = lax.broadcasted_iota(jnp.int32, (slots, attended.shape[1]), 1) // DH
    total = attended[:slots]
    for h in range(1, heads):
        total = jnp.where(head_of == h, attended[h * slots : (h + 1) * slots], total)
    return total.astype(BF16)


def bias_kernel(parents_ref, counts_ref, buckets_ref, table_ref, out_ref):
    for r, bias in enumerate(draft_biases(parents_ref, counts_ref, buckets_ref, table_ref)):
        out_ref[r] = bias


def bias_and_mask(parents, counts, buckets, bias_table):
    requests, slots = parents.shape
    heads = bias_table.shape[1]
    return pl.pallas_call(
        bias_kernel,
        out_shape=jax.ShapeDtypeStruct((requests, heads * slots, slots), F32),
        in_specs=[VMEM, SMEM, VMEM, VMEM],
        out_specs=VMEM,
        compiler_params=params(60),
        cost_estimate=cost(6e7, 1.2e6),
        name="bias_and_mask",
    )(parents, counts, buckets, bias_table.T)


def self_kernel(length_ref, qkv_ref, cache_ref, bias_ref, out_ref):
    step, width = out_ref.shape[0], out_ref.shape[2]
    heads = width // DH
    position = lax.broadcasted_iota(jnp.int32, (1, cache_ref.shape[2]), 1)
    for s in range(step):
        length = length_ref[pl.program_id(0) * step + s]
        queries = spread_heads(qkv_ref[0, s], heads)
        scores = dot_nt(queries, cache_ref[s, 0])
        scores = jnp.where(position < length, scores, NEG)
        draft = dot_nt(queries, qkv_ref[1, s]) + bias_ref[s]
        highest = jnp.maximum(scores.max(-1, keepdims=True), draft.max(-1, keepdims=True))
        scores = jnp.exp(scores - highest)
        draft = jnp.exp(draft - highest)
        total = scores.sum(-1, keepdims=True) + draft.sum(-1, keepdims=True)
        attended = dot(scores.astype(BF16), cache_ref[s, 1])
        attended = attended + dot(draft.astype(BF16), qkv_ref[2, s])
        out_ref[s] = gather_heads(attended / total, heads)


def self_attention(draft_qkv, cache, length, bias):
    _, requests, slots, width = draft_qkv.shape
    step = requests // HALVES
    depth = cache.shape[2]
    return pl.pallas_call(
        self_kernel,
        grid=(HALVES,),
        out_shape=jax.ShapeDtypeStruct((requests, slots, width), BF16),
        in_specs=[
            SMEM,
            pl.BlockSpec((3, step, slots, width), lambda h: (0, h, 0, 0)),
            pl.BlockSpec((step, 2, depth, width), lambda h: (h, 0, 0, 0)),
            pl.BlockSpec((step, bias.shape[1], slots), lambda h: (h, 0, 0)),
        ],
        out_specs=pl.BlockSpec((step, slots, width), lambda h: (h, 0, 0)),
        compiler_params=params(60),
        cost_estimate=cost(5e9, 6e6, 1.2e6),
        name="self_attention",
    )(length, draft_qkv, cache, bias)


def columns(ref, pieces, j):
    lanes = ref.shape[-1] // pieces
    return pl.ds(pl.multiple_of(jnp.bitwise_xor(lax.axis_index("tok"), j) * lanes, lanes), lanes)


def each_slice(stacks, orders):
    for stack, order in zip(stacks, orders):
        for at, k in enumerate(order):
            yield k, stack.at[at]


def join_columns(out_ref, slices, first, rows):
    for k, piece in slices:
        lanes = piece.shape[1]
        out_ref[:, k * lanes : (k + 1) * lanes] = piece[first : first + rows, :]


def self_out_kernel(ways, orders, first, *refs):
    stacks = refs[: len(orders)]
    ctx_ref, hidden_ref, own_ref = refs[len(orders) : len(orders) + 3]
    out_refs = refs[-ways:-1]
    w_ref = refs[-1]
    pieces = sum(len(order) for order in orders)
    width = ctx_ref.shape[2]
    share, model = hidden_ref.shape[1:]
    rows = own_ref.shape[0]
    requests = rows // share
    join_columns(w_ref, each_slice(stacks, orders), 0, width)
    taken = []
    for k in range(ways):
        owner = jnp.bitwise_xor(lax.axis_index("grp"), k)
        start = pl.multiple_of(owner * share, share)
        taken.append(
            ctx_ref[first : first + requests, pl.ds(start, share), :].reshape(rows, width)
        )
    part = dot(jnp.concatenate(taken, axis=0), w_ref[...])
    for k in range(1, ways):
        out_refs[k - 1][...] = part[k * rows : (k + 1) * rows].astype(BF16)
    lanes = model // pieces
    for j in range(pieces):
        base = hidden_ref[first : first + requests, :, columns(hidden_ref, pieces, j)]
        here = slice(j * lanes, (j + 1) * lanes)
        own_ref[:, here] = part[:rows, here] + base.astype(F32).reshape(rows, lanes)


def self_out(ctx, stacks, orders, hidden, ways, first, count):
    width = ctx.shape[2]
    share, model = hidden.shape[1:]
    rows = count * share
    return pl.pallas_call(
        functools.partial(self_out_kernel, ways, orders, first),
        out_shape=[jax.ShapeDtypeStruct((rows, model), F32)]
        + [jax.ShapeDtypeStruct((rows, model), BF16)] * (ways - 1),
        in_specs=[VMEM] * (len(stacks) + 2),
        out_specs=[VMEM] * ways,
        scratch_shapes=[pltpu.VMEM((width, model), BF16)],
        compiler_params=params(),
        cost_estimate=cost(2 * rows * ways * width * model, 2e6),
        name="self_out",
    )(*stacks, ctx, hidden)


def norm_kernel(pieces, last, own_ref, *refs):
    others = refs[:-3]
    gain_ref, stream_ref, normed_ref = refs[-3:]
    stream = own_ref[...]
    for other in others:
        stream = stream + other[...].astype(F32)
    lanes = stream.shape[1] // pieces
    scale = lax.rsqrt(jnp.mean(stream * stream, axis=-1, keepdims=True) + 1e-06)
    for j in range(pieces):
        here = slice(j * lanes, (j + 1) * lanes)
        there = columns(gain_ref, pieces, j)
        stream_ref[:, there if last else here] = stream[:, here].astype(stream_ref.dtype)
        normed_ref[:, here] = (stream[:, here] * scale * gain_ref[:, there]).astype(BF16)


def norm(own, others, gain, pieces, last=False):
    return pl.pallas_call(
        functools.partial(norm_kernel, pieces, last),
        out_shape=[
            jax.ShapeDtypeStruct(own.shape, BF16 if last else F32),
            jax.ShapeDtypeStruct(own.shape, BF16),
        ],
        in_specs=[VMEM] * (len(others) + 2),
        out_specs=[VMEM] * 2,
        compiler_params=params(),
        cost_estimate=cost(1e6, 2e6),
        name="norm",
    )(own, *others, gain.reshape(1, -1))


def cross_kernel(ways, orders, first, length_ref, cache_ref, stream_ref, *refs):
    blocks = refs[:ways]
    given = refs[ways : -(ways + 2)]
    own_ref = refs[-(ways + 2)]
    out_refs = refs[-(ways + 1) : -2]
    wq_ref, ctx_ref = refs[-2:]
    requests = cache_ref.shape[0]
    width = wq_ref.shape[1]
    heads = width // DH
    rows = blocks[0].shape[0]
    share = rows // requests
    wo_ref = given[-1]
    if orders:
        pieces, _, lanes = given[0].shape
        for k in range(pieces):
            piece = given[0].at[jnp.bitwise_xor(lax.axis_index("tok"), k)]
            for c in range(width // lanes):
                here = slice(c * lanes, (c + 1) * lanes)
                block = piece[c * lanes : (c + 1) * lanes, :]
                wq_ref[k * lanes : (k + 1) * lanes, here] = block
    else:
        wq_ref[...] = given[0][...]
    normed = jnp.concatenate([block[...] for block in blocks], axis=0)
    query = dot(normed, wq_ref[...]).astype(BF16).reshape(ways, rows, width)
    position = lax.broadcasted_iota(jnp.int32, (1, cache_ref.shape[2]), 1)
    for r in range(requests):
        here = slice(r * share, (r + 1) * share)
        queries = spread_heads(query[:, here].reshape(ways * share, width), heads)
        scores = dot_nt(queries, cache_ref[r, 0])
        scores = jnp.where(position < length_ref[first + r], scores, NEG)
        scores = jnp.exp(scores - scores.max(-1, keepdims=True))
        total = scores.sum(-1, keepdims=True)
        attended = dot(scores.astype(BF16), cache_ref[r, 1])
        ctx = gather_heads(attended / total, heads)
        ctx_ref[:, here, :] = ctx.reshape(ways, share, width)
    part = dot(ctx_ref[...].reshape(ways * rows, width), wo_ref[...])
    own_ref[...] = part[:rows] + stream_ref[...]
    for k in range(1, ways):
        out_refs[k - 1][...] = part[k * rows : (k + 1) * rows].astype(BF16)


def cross_layer(blocks, weights, orders, cache, stream, length, first, count):
    ways = len(blocks)
    rows, model = blocks[0].shape
    depth, width = cache.shape[2:]
    full = lambda shape: pl.BlockSpec(shape, lambda i: (0,) * len(shape))
    return pl.pallas_call(
        functools.partial(cross_kernel, ways, orders, first),
        grid=(1,),
        out_shape=[jax.ShapeDtypeStruct((rows, model), F32)]
        + [jax.ShapeDtypeStruct((rows, model), BF16)] * (ways - 1),
        in_specs=[
            SMEM,
            pl.BlockSpec((count, 2, depth, width), lambda i: (first // count, 0, 0, 0)),
            full((rows, model)),
        ]
        + [full((rows, model))] * ways
        + [full(weight.shape) for weight in weights],
        out_specs=[full((rows, model))] * ways,
        scratch_shapes=[
            pltpu.VMEM((model, width), BF16),
            pltpu.VMEM((ways, rows, width), BF16),
        ],
        compiler_params=params(CROSS_LIMIT),
        cost_estimate=cost(5e9 * count / 8, 8e6 * count / 8, 1.2e6 * count / 8),
        name="cross_layer",
    )(length, cache, stream, *blocks, *weights)


def join_kernel(slices_ref, *out_refs):
    pieces, _, lanes = slices_ref.shape
    for k in range(pieces):
        source = jnp.bitwise_xor(lax.axis_index("tok"), k)
        at = slices_ref.shape[1] - sum(ref.shape[0] for ref in out_refs)
        for out_ref in out_refs:
            rows = out_ref.shape[0]
            out_ref[:, k * lanes : (k + 1) * lanes] = slices_ref[source, at : at + rows, :]
            at += rows


def join(slices, *depths):
    pieces, rows, lanes = slices.shape
    return pl.pallas_call(
        join_kernel,
        out_shape=[jax.ShapeDtypeStruct((depth, lanes * pieces), BF16) for depth in depths],
        in_specs=[VMEM],
        out_specs=[VMEM] * len(depths),
        compiler_params=params(),
        cost_estimate=cost(1e3, 4 * rows * lanes * pieces),
        name="join",
    )(slices)


def ffn_kernel(ways, gate_ref, late_ref, stream_ref, *refs):
    blocks, own_ref, out_refs = refs[:ways], refs[ways], refs[ways + 1 :]
    hidden = gate_ref.shape[0]
    rows = stream_ref.shape[0]
    normed = jnp.concatenate([block[...] for block in blocks], axis=0)
    gate = dot_nt(normed, gate_ref[...])
    up = dot_nt(normed, late_ref[:hidden, :])
    gated = (jax.nn.gelu(gate, approximate=True) * up).astype(BF16)
    part = dot(gated, late_ref[hidden:, :])
    own_ref[...] = part[:rows] + stream_ref[...]
    for k in range(1, ways):
        out_refs[k - 1][...] = part[k * rows : (k + 1) * rows].astype(BF16)


def ffn(blocks, w_gate, w_late, stream):
    ways = len(blocks)
    rows, model = stream.shape
    return pl.pallas_call(
        functools.partial(ffn_kernel, ways),
        out_shape=[jax.ShapeDtypeStruct((rows, model), F32)]
        + [jax.ShapeDtypeStruct((rows, model), BF16)] * (ways - 1),
        in_specs=[VMEM] * (3 + ways),
        out_specs=[VMEM] * ways,
        compiler_params=params(),
        cost_estimate=cost(2 * rows * ways * (w_gate.size + w_late.size), 6e6, 4e5),
        name="ffn",
    )(w_gate, w_late, stream, *blocks)


def project_kernel(ways, first, slices_ref, *refs):
    blocks, out_hbm, w_ref, made_ref, sem = refs[:ways], *refs[-4:]
    _, count, slots, width = made_ref.shape
    share = slots // ways
    pieces, _, depth, _ = slices_ref.shape
    for k in range(pieces):
        source = jnp.bitwise_xor(lax.axis_index("tok"), k) if pieces > 1 else 0
        w_ref[:, k * depth : (k + 1) * depth, :] = slices_ref[source]
    normed = jnp.concatenate([block[...] for block in blocks], axis=0)
    for c in range(3):
        projected = dot(normed, w_ref[c]).astype(BF16).reshape(ways, count, share, width)
        for k in range(ways):
            start = pl.multiple_of(jnp.bitwise_xor(lax.axis_index("grp"), k) * share, share)
            made_ref[c, :, pl.ds(start, share), :] = projected[k]
    copy = pltpu.make_async_copy(made_ref, out_hbm.at[:, first : first + count], sem)
    copy.start()
    copy.wait()


def project(blocks, slices, requests, share, first, count, base):
    ways = len(blocks)
    model = blocks[0].shape[1]
    width = slices.shape[3]
    given = [] if base is None else [base]
    return pl.pallas_call(
        functools.partial(project_kernel, ways, first),
        out_shape=jax.ShapeDtypeStruct((3, requests, share * ways, width), BF16),
        in_specs=[VMEM] * (ways + 1) + [HBM] * len(given),
        out_specs=HBM,
        scratch_shapes=[
            pltpu.VMEM((3, model, width), BF16),
            pltpu.VMEM((3, count, share * ways, width), BF16),
            pltpu.SemaphoreType.DMA,
        ],
        input_output_aliases={ways + 1: 0} if given else {},
        compiler_params=params(),
        cost_estimate=cost(6 * count * share * ways * model * width, 4e6),
        name="project",
    )(slices, *blocks, *given)


ATTN_ORDERS = ((0, 4, 6, 2), (1, 5, 7, 3))


def gate(*values):
    return lax.optimization_barrier(values)


def partner(value, axis, size, k):
    return lax.ppermute(value, axis, [(i, i ^ k) for i in range(size)])


def all_slices(shard):
    return lax.all_gather(shard, "tok", axis=0, tiled=False)


def along(value, k):
    return partner(value, "tok", 8, k)


def send_each(parts, ways):
    return [partner(part, "grp", ways, k) for k, part in zip(range(1, ways), parts)]


def spread(block, ways):
    return [block] + send_each([block] * (ways - 1), ways)


def shards(
    ways,
    total,
    hidden,
    draft_qkv,
    self_cache,
    cross_cache,
    parents,
    counts,
    self_len,
    enc_len,
    buckets,
    bias_table,
    gain_cross,
    gain_ffn,
    gain_next,
    w_out_self,
    w_query_cross,
    w_out_cross,
    w_gate,
    w_up,
    w_down,
    w_qkv,
):
    requests, share, model = hidden.shape
    slice_lanes = model // total
    head_width = w_query_cross.shape[1]
    paired = total == 8 and slice_lanes == 128 and head_width % slice_lanes == 0
    qkv_shard = jnp.transpose(w_qkv, (1, 0, 2))
    halves = range(HALVES)
    count = requests // HALVES
    starts = [h * count for h in halves]
    bias = bias_and_mask(parents, counts, buckets, bias_table)
    ctx = self_attention(draft_qkv, self_cache, self_len, bias)
    if paired:
        pieces, orders, cross_orders = total, ATTN_ORDERS, ATTN_ORDERS
        query_slices = jnp.split(w_query_cross, head_width // slice_lanes, axis=1)
        early = all_slices(jnp.concatenate(query_slices + [w_out_cross, w_gate.T], axis=0))
        out_shard = w_out_self
        out_here = [out_shard] + [along(out_shard, k) for k in (4, 6, 2)]
        ctx, out_here = gate(ctx, out_here)
        out_here = jnp.stack(out_here)
        out_w = [out_here, along(out_here, 1)]
        out_here, w_up, w_down, qkv_shard = gate(out_here, w_up, w_down, qkv_shard)
        late = all_slices(jnp.concatenate([w_up.T, w_down], axis=0))
    else:
        pieces = 1
        by_row = functools.partial(lax.all_gather, axis_name="tok", axis=0, tiled=True)
        by_col = functools.partial(lax.all_gather, axis_name="tok", axis=1, tiled=True)
        out_w, orders, cross_orders = [by_col(w_out_self)[None]], ((0,),), ()
        attn_w = [by_row(w_query_cross), by_col(w_out_cross)]
        ffn_gate = by_row(w_gate).T
        ffn_late = jnp.concatenate([by_row(w_up).T, by_col(w_down)], axis=0)
        qkv_w = by_col(qkv_shard)[None]
    made = [self_out(ctx, out_w, orders, hidden, ways, start, count) for start in starts]
    if paired:
        *made[-1], qkv_shard = gate(*made[-1], qkv_shard)
        qkv_w = all_slices(qkv_shard)
    sent = [send_each(made[h][1:], ways) for h in halves]
    kept = [norm(made[h][0], sent[h], gain_cross, pieces) for h in halves]
    blocks = [spread(kept[h][1], ways) for h in halves]
    if paired:
        out_cross, ffn_gate = join(early, head_width, w_gate.shape[1])
        attn_w = [early[:, :head_width], out_cross]
    made = [
        cross_layer(
            blocks[h], attn_w, cross_orders, cross_cache, kept[h][0], enc_len, starts[h], count
        )
        for h in halves
    ]
    sent = [send_each(made[h][1:], ways) for h in halves]
    kept = [norm(made[h][0], sent[h], gain_ffn, pieces) for h in halves]
    blocks = [spread(kept[h][1], ways) for h in halves]
    if paired:
        (ffn_late,) = join(late, w_up.shape[1] + w_down.shape[0])
    made = [ffn(blocks[h], ffn_gate, ffn_late, kept[h][0]) for h in halves]
    sent = [send_each(made[h][1:], ways) for h in halves]
    kept = [norm(made[h][0], sent[h], gain_next, pieces, True) for h in halves]
    blocks = [spread(kept[h][1], ways) for h in halves]
    next_qkv = None
    for h in halves:
        next_qkv = project(blocks[h], qkv_w, requests, share, starts[h], count, next_qkv)
    out_hidden = jnp.concatenate([kept[h][0] for h in halves], axis=0)
    return out_hidden.reshape(requests, share, model), next_qkv


def solution(mesh):
    in_specs = (
        P("tok", "grp", None),
        P(None, "tok", None, "grp"),
        P("tok", None, None, "grp"),
        P("tok", None, None, "grp"),
        P("tok", None),
        P("tok"),
        P("tok"),
        P("tok"),
        P("tok", None, None),
        P(None, "grp"),
        P(),
        P(),
        P(),
        P("grp", "tok"),
        P("tok", "grp"),
        P("grp", "tok"),
        P("tok", "grp"),
        P("tok", "grp"),
        P("grp", "tok"),
        P("tok", None, "grp"),
    )
    out_specs = (P("tok", "grp", None), P(None, "tok", None, "grp"))
    body = functools.partial(shards, mesh.shape["grp"], mesh.shape["tok"])
    return jax.shard_map(body, mesh=mesh, in_specs=in_specs, out_specs=out_specs, check_vma=False)
```

```python
import functools
import jax
import jax.numpy as jnp
from jax import lax
from jax.experimental import pallas as pl
from jax.experimental.pallas import tpu as pltpu
from jax.sharding import PartitionSpec as P

DH = 64
HALVES = 2
F32 = jnp.float32
BF16 = jnp.bfloat16
NEG = -1e30
MIB = 1024 * 1024
CROSS_LIMIT = 28
HBM = pl.BlockSpec(memory_space=pl.ANY)
SMEM = pl.BlockSpec(memory_space=pltpu.SMEM)
VMEM = pl.BlockSpec(memory_space=pltpu.VMEM)


def params(limit=28):
    return pltpu.CompilerParams(vmem_limit_bytes=limit * MIB)


def cost(flops, moved, transcendentals=0):
    return pl.CostEstimate(
        flops=int(flops), bytes_accessed=int(moved), transcendentals=int(transcendentals)
    )


def dot_nt(lhs, rhs):
    return lax.dot_general(lhs, rhs, (((1,), (1,)), ((), ())), preferred_element_type=F32)


def dot(lhs, rhs):
    return jnp.dot(lhs, rhs, preferred_element_type=F32)


def ancestor_masks(parents_ref, counts_ref):
    requests, slots = parents_ref.shape
    row = lax.broadcasted_iota(jnp.int32, (slots, slots), 0)
    col = lax.broadcasted_iota(jnp.int32, (slots, slots), 1)
    reach = []
    for r in range(requests):
        linked = (row == parents_ref[r : r + 1, :]) | (row == col)
        reach.append(jnp.where(linked, 1.0, 0.0).astype(BF16))
    span = 1
    while span < slots - 1:
        reach = [jnp.minimum(dot(a, a), 1.0).astype(BF16) for a in reach]
        span *= 2
    eye = jnp.where(row == col, 1.0, 0.0).astype(BF16)
    return [(dot_nt(eye, reach[r]) > 0.5) & (col < counts_ref[r]) for r in range(requests)]


def draft_biases(parents_ref, counts_ref, buckets_ref, table_ref):
    requests, slots = parents_ref.shape
    heads, kinds = table_ref.shape
    lanes = 2 * slots
    live = ancestor_masks(parents_ref, counts_ref)
    shifted = table_ref[...] - table_ref[:, kinds - 1 :]
    table = jnp.concatenate([shifted, jnp.zeros((heads, lanes - kinds), F32)], axis=1)
    biases = [[] for _ in range(requests)]
    for r in range(0, requests, 2):
        picked = jnp.concatenate([buckets_ref[r], buckets_ref[r + 1]], axis=1)
        for h in range(heads):
            row_of = jnp.broadcast_to(table[h : h + 1, :], (slots, lanes))
            both = jnp.take_along_axis(row_of, picked, axis=1)
            biases[r].append(jnp.where(live[r], both[:, :slots], NEG))
            biases[r + 1].append(jnp.where(live[r + 1], both[:, slots:], NEG))
    return [jnp.concatenate(parts, axis=0) for parts in biases]


def spread_heads(queries, heads):
    head_of = lax.broadcasted_iota(jnp.int32, queries.shape, 1) // DH
    return jnp.concatenate(
        [jnp.where(head_of == h, queries, jnp.zeros_like(queries)) for h in range(heads)], axis=0
    )


def gather_heads(attended, heads):
    slots = attended.shape[0] // heads
    head_of = lax.broadcasted_iota(jnp.int32, (slots, attended.shape[1]), 1) // DH
    total = attended[:slots]
    for h in range(1, heads):
        total = jnp.where(head_of == h, attended[h * slots : (h + 1) * slots], total)
    return total.astype(BF16)


def bias_kernel(parents_ref, counts_ref, buckets_ref, table_ref, out_ref):
    for r, bias in enumerate(draft_biases(parents_ref, counts_ref, buckets_ref, table_ref)):
        out_ref[r] = bias


def bias_and_mask(parents, counts, buckets, bias_table):
    requests, slots = parents.shape
    heads = bias_table.shape[1]
    return pl.pallas_call(
        bias_kernel,
        out_shape=jax.ShapeDtypeStruct((requests, heads * slots, slots), F32),
        in_specs=[VMEM, SMEM, VMEM, VMEM],
        out_specs=VMEM,
        compiler_params=params(60),
        cost_estimate=cost(6e7, 1.2e6),
        name="bias_and_mask",
    )(parents, counts, buckets, bias_table.T)


def self_kernel(length_ref, qkv_ref, cache_ref, bias_ref, out_ref):
    step, width = out_ref.shape[0], out_ref.shape[2]
    heads = width // DH
    position = lax.broadcasted_iota(jnp.int32, (1, cache_ref.shape[2]), 1)
    for s in range(step):
        length = length_ref[pl.program_id(0) * step + s]
        queries = spread_heads(qkv_ref[0, s], heads)
        scores = dot_nt(queries, cache_ref[s, 0])
        scores = jnp.where(position < length, scores, NEG)
        draft = dot_nt(queries, qkv_ref[1, s]) + bias_ref[s]
        highest = jnp.maximum(scores.max(-1, keepdims=True), draft.max(-1, keepdims=True))
        scores = jnp.exp(scores - highest)
        draft = jnp.exp(draft - highest)
        total = scores.sum(-1, keepdims=True) + draft.sum(-1, keepdims=True)
        attended = dot(scores.astype(BF16), cache_ref[s, 1])
        attended = attended + dot(draft.astype(BF16), qkv_ref[2, s])
        out_ref[s] = gather_heads(attended / total, heads)


def self_attention(draft_qkv, cache, length, bias):
    _, requests, slots, width = draft_qkv.shape
    step = requests // HALVES
    depth = cache.shape[2]
    return pl.pallas_call(
        self_kernel,
        grid=(HALVES,),
        out_shape=jax.ShapeDtypeStruct((requests, slots, width), BF16),
        in_specs=[
            SMEM,
            pl.BlockSpec((3, step, slots, width), lambda h: (0, h, 0, 0)),
            pl.BlockSpec((step, 2, depth, width), lambda h: (h, 0, 0, 0)),
            pl.BlockSpec((step, bias.shape[1], slots), lambda h: (h, 0, 0)),
        ],
        out_specs=pl.BlockSpec((step, slots, width), lambda h: (h, 0, 0)),
        compiler_params=params(60),
        cost_estimate=cost(5e9, 6e6, 1.2e6),
        name="self_attention",
    )(length, draft_qkv, cache, bias)


def columns(ref, pieces, j):
    lanes = ref.shape[-1] // pieces
    return pl.ds(pl.multiple_of(jnp.bitwise_xor(lax.axis_index("tok"), j) * lanes, lanes), lanes)


def each_slice(stacks, orders):
    for stack, order in zip(stacks, orders):
        for at, k in enumerate(order):
            yield k, stack.at[at]


def join_columns(out_ref, slices, first, rows):
    for k, piece in slices:
        lanes = piece.shape[1]
        out_ref[:, k * lanes : (k + 1) * lanes] = piece[first : first + rows, :]


def self_out_kernel(ways, orders, first, *refs):
    stacks = refs[: len(orders)]
    ctx_ref, hidden_ref, own_ref = refs[len(orders) : len(orders) + 3]
    out_refs = refs[-ways:-1]
    w_ref = refs[-1]
    pieces = sum(len(order) for order in orders)
    width = ctx_ref.shape[2]
    share, model = hidden_ref.shape[1:]
    rows = own_ref.shape[0]
    requests = rows // share
    join_columns(w_ref, each_slice(stacks, orders), 0, width)
    taken = []
    for k in range(ways):
        owner = jnp.bitwise_xor(lax.axis_index("grp"), k)
        start = pl.multiple_of(owner * share, share)
        taken.append(
            ctx_ref[first : first + requests, pl.ds(start, share), :].reshape(rows, width)
        )
    part = dot(jnp.concatenate(taken, axis=0), w_ref[...])
    for k in range(1, ways):
        out_refs[k - 1][...] = part[k * rows : (k + 1) * rows].astype(BF16)
    lanes = model // pieces
    for j in range(pieces):
        base = hidden_ref[first : first + requests, :, columns(hidden_ref, pieces, j)]
        here = slice(j * lanes, (j + 1) * lanes)
        own_ref[:, here] = part[:rows, here] + base.astype(F32).reshape(rows, lanes)


def self_out(ctx, stacks, orders, hidden, ways, first, count):
    width = ctx.shape[2]
    share, model = hidden.shape[1:]
    rows = count * share
    return pl.pallas_call(
        functools.partial(self_out_kernel, ways, orders, first),
        out_shape=[jax.ShapeDtypeStruct((rows, model), F32)]
        + [jax.ShapeDtypeStruct((rows, model), BF16)] * (ways - 1),
        in_specs=[VMEM] * (len(stacks) + 2),
        out_specs=[VMEM] * ways,
        scratch_shapes=[pltpu.VMEM((width, model), BF16)],
        compiler_params=params(),
        cost_estimate=cost(2 * rows * ways * width * model, 2e6),
        name="self_out",
    )(*stacks, ctx, hidden)


def norm_kernel(pieces, last, own_ref, *refs):
    others = refs[:-3]
    gain_ref, stream_ref, normed_ref = refs[-3:]
    stream = own_ref[...]
    for other in others:
        stream = stream + other[...].astype(F32)
    lanes = stream.shape[1] // pieces
    scale = lax.rsqrt(jnp.mean(stream * stream, axis=-1, keepdims=True) + 1e-06)
    for j in range(pieces):
        here = slice(j * lanes, (j + 1) * lanes)
        there = columns(gain_ref, pieces, j)
        stream_ref[:, there if last else here] = stream[:, here].astype(stream_ref.dtype)
        normed_ref[:, here] = (stream[:, here] * scale * gain_ref[:, there]).astype(BF16)


def norm(own, others, gain, pieces, last=False):
    return pl.pallas_call(
        functools.partial(norm_kernel, pieces, last),
        out_shape=[
            jax.ShapeDtypeStruct(own.shape, BF16 if last else F32),
            jax.ShapeDtypeStruct(own.shape, BF16),
        ],
        in_specs=[VMEM] * (len(others) + 2),
        out_specs=[VMEM] * 2,
        compiler_params=params(),
        cost_estimate=cost(1e6, 2e6),
        name="norm",
    )(own, *others, gain.reshape(1, -1))


def cross_kernel(ways, first, length_ref, cache_ref, stream_ref, *refs):
    blocks = refs[:ways]
    given = refs[ways : -(ways + 1)]
    own_ref = refs[-(ways + 1)]
    out_refs = refs[-ways:-1]
    ctx_ref = refs[-1]
    wq_ref, wo_ref = given
    requests = cache_ref.shape[0]
    width = wq_ref.shape[1]
    heads = width // DH
    rows = blocks[0].shape[0]
    share = rows // requests
    normed = jnp.concatenate([block[...] for block in blocks], axis=0)
    query = dot(normed, wq_ref[...]).astype(BF16).reshape(ways, rows, width)
    position = lax.broadcasted_iota(jnp.int32, (1, cache_ref.shape[2]), 1)
    for r in range(requests):
        here = slice(r * share, (r + 1) * share)
        queries = spread_heads(query[:, here].reshape(ways * share, width), heads)
        scores = dot_nt(queries, cache_ref[r, 0])
        scores = jnp.where(position < length_ref[first + r], scores, NEG)
        scores = jnp.exp(scores - scores.max(-1, keepdims=True))
        total = scores.sum(-1, keepdims=True)
        attended = dot(scores.astype(BF16), cache_ref[r, 1])
        ctx = gather_heads(attended / total, heads)
        ctx_ref[:, here, :] = ctx.reshape(ways, share, width)
    part = dot(ctx_ref[...].reshape(ways * rows, width), wo_ref[...])
    own_ref[...] = part[:rows] + stream_ref[...]
    for k in range(1, ways):
        out_refs[k - 1][...] = part[k * rows : (k + 1) * rows].astype(BF16)


def cross_layer(blocks, weights, cache, stream, length, first, count):
    ways = len(blocks)
    rows, model = blocks[0].shape
    depth, width = cache.shape[2:]
    full = lambda shape: pl.BlockSpec(shape, lambda i: (0,) * len(shape))
    return pl.pallas_call(
        functools.partial(cross_kernel, ways, first),
        grid=(1,),
        out_shape=[jax.ShapeDtypeStruct((rows, model), F32)]
        + [jax.ShapeDtypeStruct((rows, model), BF16)] * (ways - 1),
        in_specs=[
            SMEM,
            pl.BlockSpec((count, 2, depth, width), lambda i: (first // count, 0, 0, 0)),
            full((rows, model)),
        ]
        + [full((rows, model))] * ways
        + [full(weight.shape) for weight in weights],
        out_specs=[full((rows, model))] * ways,
        scratch_shapes=[
            pltpu.VMEM((ways, rows, width), BF16),
        ],
        compiler_params=params(CROSS_LIMIT),
        cost_estimate=cost(5e9 * count / 8, 8e6 * count / 8, 1.2e6 * count / 8),
        name="cross_layer",
    )(length, cache, stream, *blocks, *weights)


def join_kernel(query, slices_ref, *out_refs):
    pieces, _, lanes = slices_ref.shape
    for k in range(pieces):
        source = jnp.bitwise_xor(lax.axis_index("tok"), k)
        at = 0
        for n, out_ref in enumerate(out_refs):
            if query and n == 0:
                for c in range(out_ref.shape[1] // lanes):
                    block = slices_ref[source, at : at + lanes, :]
                    here = slice(c * lanes, (c + 1) * lanes)
                    out_ref[k * lanes : (k + 1) * lanes, here] = block
                    at += lanes
            else:
                rows = out_ref.shape[0]
                out_ref[:, k * lanes : (k + 1) * lanes] = slices_ref[source, at : at + rows, :]
                at += rows


def join(slices, query, *depths):
    pieces, rows, lanes = slices.shape
    shapes = [(depth, lanes * pieces) for depth in depths]
    if query:
        shapes = [(lanes * pieces, query)] + shapes
    return pl.pallas_call(
        functools.partial(join_kernel, query),
        out_shape=[jax.ShapeDtypeStruct(shape, BF16) for shape in shapes],
        in_specs=[VMEM],
        out_specs=[VMEM] * len(shapes),
        compiler_params=params(),
        cost_estimate=cost(1e3, 4 * rows * lanes * pieces),
        name="join",
    )(slices)


def ffn_kernel(ways, gate_ref, late_ref, stream_ref, *refs):
    blocks, own_ref, out_refs = refs[:ways], refs[ways], refs[ways + 1 :]
    hidden = gate_ref.shape[0]
    rows = stream_ref.shape[0]
    normed = jnp.concatenate([block[...] for block in blocks], axis=0)
    gate = dot_nt(normed, gate_ref[...])
    up = dot_nt(normed, late_ref[:hidden, :])
    gated = (jax.nn.gelu(gate, approximate=True) * up).astype(BF16)
    part = dot(gated, late_ref[hidden:, :])
    own_ref[...] = part[:rows] + stream_ref[...]
    for k in range(1, ways):
        out_refs[k - 1][...] = part[k * rows : (k + 1) * rows].astype(BF16)


def ffn(blocks, w_gate, w_late, stream):
    ways = len(blocks)
    rows, model = stream.shape
    return pl.pallas_call(
        functools.partial(ffn_kernel, ways),
        out_shape=[jax.ShapeDtypeStruct((rows, model), F32)]
        + [jax.ShapeDtypeStruct((rows, model), BF16)] * (ways - 1),
        in_specs=[VMEM] * (3 + ways),
        out_specs=[VMEM] * ways,
        compiler_params=params(),
        cost_estimate=cost(2 * rows * ways * (w_gate.size + w_late.size), 6e6, 4e5),
        name="ffn",
    )(w_gate, w_late, stream, *blocks)


def project_kernel(ways, first, slices_ref, *refs):
    blocks, out_hbm, w_ref, made_ref, sem = refs[:ways], *refs[-4:]
    _, count, slots, width = made_ref.shape
    share = slots // ways
    pieces, _, depth, _ = slices_ref.shape
    for k in range(pieces):
        source = jnp.bitwise_xor(lax.axis_index("tok"), k) if pieces > 1 else 0
        w_ref[:, k * depth : (k + 1) * depth, :] = slices_ref[source]
    normed = jnp.concatenate([block[...] for block in blocks], axis=0)
    for c in range(3):
        projected = dot(normed, w_ref[c]).astype(BF16).reshape(ways, count, share, width)
        for k in range(ways):
            start = pl.multiple_of(jnp.bitwise_xor(lax.axis_index("grp"), k) * share, share)
            made_ref[c, :, pl.ds(start, share), :] = projected[k]
    copy = pltpu.make_async_copy(made_ref, out_hbm.at[:, first : first + count], sem)
    copy.start()
    copy.wait()


def project(blocks, slices, requests, share, first, count, base):
    ways = len(blocks)
    model = blocks[0].shape[1]
    width = slices.shape[3]
    given = [] if base is None else [base]
    return pl.pallas_call(
        functools.partial(project_kernel, ways, first),
        out_shape=jax.ShapeDtypeStruct((3, requests, share * ways, width), BF16),
        in_specs=[VMEM] * (ways + 1) + [HBM] * len(given),
        out_specs=HBM,
        scratch_shapes=[
            pltpu.VMEM((3, model, width), BF16),
            pltpu.VMEM((3, count, share * ways, width), BF16),
            pltpu.SemaphoreType.DMA,
        ],
        input_output_aliases={ways + 1: 0} if given else {},
        compiler_params=params(),
        cost_estimate=cost(6 * count * share * ways * model * width, 4e6),
        name="project",
    )(slices, *blocks, *given)


ATTN_ORDERS = ((0, 4, 6, 2), (1, 5, 7, 3))


def gate(*values):
    return lax.optimization_barrier(values)


def partner(value, axis, size, k):
    return lax.ppermute(value, axis, [(i, i ^ k) for i in range(size)])


def all_slices(shard):
    return lax.all_gather(shard, "tok", axis=0, tiled=False)


def pack_kernel(query_ref, *refs):
    early_ref, late_ref = refs[-2:]
    lanes = early_ref.shape[1]
    at = 0
    for c in range(query_ref.shape[1] // lanes):
        early_ref[at : at + lanes, :] = query_ref[:, c * lanes : (c + 1) * lanes]
        at += lanes
    for ref in refs[:2]:
        early_ref[at : at + ref.shape[0], :] = ref[...]
        at += ref.shape[0]
    at = 0
    for ref in refs[2:4]:
        late_ref[at : at + ref.shape[0], :] = ref[...]
        at += ref.shape[0]


def pack(query, out, w_gate, w_up, w_down):
    lanes = out.shape[1]
    early = query.size // lanes + out.shape[0] + w_gate.shape[1]
    late = w_up.shape[1] + w_down.shape[0]
    return pl.pallas_call(
        pack_kernel,
        out_shape=[jax.ShapeDtypeStruct((rows, lanes), BF16) for rows in (early, late)],
        in_specs=[VMEM] * 5,
        out_specs=[VMEM] * 2,
        compiler_params=params(60),
        cost_estimate=cost(1e3, 2e6),
        name="pack",
    )(query, out, w_gate.T, w_up.T, w_down)


def along(value, k):
    return partner(value, "tok", 8, k)


def send_each(parts, ways):
    return [partner(part, "grp", ways, k) for k, part in zip(range(1, ways), parts)]


def spread(block, ways):
    return [block] + send_each([block] * (ways - 1), ways)


def shards(
    ways,
    total,
    hidden,
    draft_qkv,
    self_cache,
    cross_cache,
    parents,
    counts,
    self_len,
    enc_len,
    buckets,
    bias_table,
    gain_cross,
    gain_ffn,
    gain_next,
    w_out_self,
    w_query_cross,
    w_out_cross,
    w_gate,
    w_up,
    w_down,
    w_qkv,
):
    requests, share, model = hidden.shape
    slice_lanes = model // total
    head_width = w_query_cross.shape[1]
    paired = total == 8 and slice_lanes == 128 and head_width % slice_lanes == 0
    qkv_shard = jnp.transpose(w_qkv, (1, 0, 2))
    halves = range(HALVES)
    count = requests // HALVES
    starts = [h * count for h in halves]
    bias = bias_and_mask(parents, counts, buckets, bias_table)
    ctx = self_attention(draft_qkv, self_cache, self_len, bias)
    if paired:
        pieces, orders = total, ATTN_ORDERS
        early, late = pack(w_query_cross, w_out_cross, w_gate, w_up, w_down)
        early = all_slices(early)
        out_shard = w_out_self
        out_here = [out_shard] + [along(out_shard, k) for k in (4, 6, 2)]
        ctx, out_here = gate(ctx, out_here)
        out_here = jnp.stack(out_here)
        out_w = [out_here, along(out_here, 1)]
        out_here, late, qkv_shard = gate(out_here, late, qkv_shard)
        late = all_slices(late)
    else:
        pieces = 1
        by_row = functools.partial(lax.all_gather, axis_name="tok", axis=0, tiled=True)
        by_col = functools.partial(lax.all_gather, axis_name="tok", axis=1, tiled=True)
        out_w, orders = [by_col(w_out_self)[None]], ((0,),)
        attn_w = [by_row(w_query_cross), by_col(w_out_cross)]
        ffn_gate = by_row(w_gate).T
        ffn_late = jnp.concatenate([by_row(w_up).T, by_col(w_down)], axis=0)
        qkv_w = by_col(qkv_shard)[None]
    made = [self_out(ctx, out_w, orders, hidden, ways, start, count) for start in starts]
    if paired:
        *made[-1], qkv_shard = gate(*made[-1], qkv_shard)
        qkv_w = all_slices(qkv_shard)
    sent = [send_each(made[h][1:], ways) for h in halves]
    kept = [norm(made[h][0], sent[h], gain_cross, pieces) for h in halves]
    blocks = [spread(kept[h][1], ways) for h in halves]
    if paired:
        query, out_cross, ffn_gate = join(early, head_width, head_width, w_gate.shape[1])
        attn_w = [query, out_cross]
    made = [
        cross_layer(
            blocks[h], attn_w, cross_cache, kept[h][0], enc_len, starts[h], count
        )
        for h in halves
    ]
    sent = [send_each(made[h][1:], ways) for h in halves]
    kept = [norm(made[h][0], sent[h], gain_ffn, pieces) for h in halves]
    blocks = [spread(kept[h][1], ways) for h in halves]
    if paired:
        (ffn_late,) = join(late, 0, w_up.shape[1] + w_down.shape[0])
    made = [ffn(blocks[h], ffn_gate, ffn_late, kept[h][0]) for h in halves]
    sent = [send_each(made[h][1:], ways) for h in halves]
    kept = [norm(made[h][0], sent[h], gain_next, pieces, True) for h in halves]
    blocks = [spread(kept[h][1], ways) for h in halves]
    next_qkv = None
    for h in halves:
        next_qkv = project(blocks[h], qkv_w, requests, share, starts[h], count, next_qkv)
    out_hidden = jnp.concatenate([kept[h][0] for h in halves], axis=0)
    return out_hidden.reshape(requests, share, model), next_qkv


def solution(mesh):
    in_specs = (
        P("tok", "grp", None),
        P(None, "tok", None, "grp"),
        P("tok", None, None, "grp"),
        P("tok", None, None, "grp"),
        P("tok", None),
        P("tok"),
        P("tok"),
        P("tok"),
        P("tok", None, None),
        P(None, "grp"),
        P(),
        P(),
        P(),
        P("grp", "tok"),
        P("tok", "grp"),
        P("grp", "tok"),
        P("tok", "grp"),
        P("tok", "grp"),
        P("grp", "tok"),
        P("tok", None, "grp"),
    )
    out_specs = (P("tok", "grp", None), P(None, "tok", None, "grp"))
    body = functools.partial(shards, mesh.shape["grp"], mesh.shape["tok"])
    return jax.shard_map(body, mesh=mesh, in_specs=in_specs, out_specs=out_specs, check_vma=False)
```
